512 devices in a mesh: group: 2 (over core), dp: 32 (over y, x), mp: 8 (over z).
Axes of the slice: x: 4, y: 8, z: 8, core: 2. Of those that a mesh axis runs over, the one named last changes fastest.
Arguments:
- teacher_hidden: bfloat16 [65536, 4096], P(('group', 'dp'), 'mp'), may hold values from -60 to 60
- teacher_gain: float32 [4096], replicated, may hold values from 0.5 to 1.5
- projector: bfloat16 [4096, 3584], P('dp', 'mp'), may hold values from -0.09375 to 0.09375
- live: int32 [65536], P(('group', 'dp')), may hold values from 0 to 1, as said below
- placement: int32 [65536], P(('group', 'dp')), may hold values from 0 to 31
- student_hidden: bfloat16 [65536, 3584], P(('group', 'dp', 'mp')), may hold values from -60 to 60
- student_gain: float32 [3584], P('mp'), may hold values from 0.5 to 1.5
Outputs:
- grad_hidden: bfloat16 [65536, 3584], P(('group', 'dp', 'mp'))
- grad_gain: float32 [3584], P('mp')
- mean_loss: float32 [], replicated
The draws below stay inside these ranges and needn't reach their ends.
Inputs may be any that keep to these rules, and one draw needn't show every extreme that they name: For each g and m, in every block of 128 teacher rows starting at ((g * 32 + d) * 8 + m) * 128, at most 4 live rows name the same placement, and for each g and m one placement value is named by exactly 4 live rows of every block of that g and m.
All inputs are finite; a program needn't handle non-finite values.
Results may differ from the reference program's by a relative error of at most 0.0057.
Values may be sent and summed in bfloat16 or wider, within the bound.
No kernel may reach another device: no remote copies, remote signals or barrier semaphores. Data moves between devices by JAX's collectives and lax.ppermute only.
A program may use at most 64 MiB of HBM per device.

```python
import math
import jax
import jax.numpy as jnp
from jax import lax

DT = 4096
DS = 3584
TOK_DEV = 128
CAP = 4
TOKENS = 65536
N_GROUP = 2
N_DP = 32
N_MP = 8


def routing_tables(key):
    k_count, k_full, k_order, k_spare = jax.random.split(key, 4)
    classes = TOKENS // (N_DP * TOK_DEV)
    groups = classes // N_MP
    counts = jax.random.randint(k_count, (classes, N_DP, N_DP), 0, CAP + 1)
    chosen = jax.random.randint(k_full, (classes, 1, 1), 0, N_DP)
    counts = jnp.where(jnp.arange(N_DP)[None, None, :] == chosen, CAP, counts)
    scores = jax.random.randint(k_order, (classes, N_DP, TOK_DEV), 0, 1 << 20) * TOK_DEV + jnp.arange(TOK_DEV)
    position = jnp.argsort(jnp.argsort(scores, axis=-1), axis=-1)
    bounds = jnp.cumsum(counts, axis=-1)
    shard_ids = jnp.sum((position[..., None] >= bounds[..., None, :]).astype(jnp.int32), axis=-1)
    live_rows = position < bounds[..., -1:]
    spare = jax.random.randint(k_spare, (classes, N_DP, TOK_DEV), 0, N_DP)
    shard_ids = jnp.where(live_rows, shard_ids, spare)

    def arrange(table):
        return table.reshape(groups, N_MP, N_DP, TOK_DEV).transpose(0, 2, 1, 3).reshape(-1).astype(jnp.int32)
    return (arrange(live_rows.astype(jnp.int32)), arrange(shard_ids))


def row_column_scales(key, row_count, columns):
    k_row, k_column = jax.random.split(key)
    row_scale = jnp.exp(jax.random.uniform(k_row, (row_count, 1), jnp.float32, math.log(0.3), math.log(3.0)))
    column_scale = jnp.exp(jax.random.uniform(k_column, (1, columns), jnp.float32, math.log(0.5), math.log(5.0)))
    return row_scale * column_scale


def draw_live(key, part):
    return routing_tables(key)[0]


def draw_placement(key, part):
    return routing_tables(key)[1]


def draw_teacher_hidden(key, part):
    key = jax.random.fold_in(key, 17)
    k_scale, k_base = jax.random.split(key, 2)
    base = jnp.clip(jax.random.normal(k_base, (TOKENS, DT), jnp.float32), -4.0, 4.0)
    return (base * row_column_scales(k_scale, TOKENS, DT)).astype(jnp.bfloat16)


def draw_student_hidden(key, part):
    key = jax.random.fold_in(key, 23)
    k_scale, k_base = jax.random.split(key, 2)
    base = jnp.clip(jax.random.normal(k_base, (TOKENS, DS), jnp.float32), -4.0, 4.0)
    return (base * row_column_scales(k_scale, TOKENS, DS)).astype(jnp.bfloat16)


def shard_levels(rng, shape, shards, low, largest):
    loudness = 1.0
    for axis_at, shards_of in shards:
        steps = jax.random.uniform(jax.random.fold_in(jax.random.fold_in(rng, 6), axis_at), (shards_of,), jnp.float32, low / len(shards), largest / len(shards))
        loudness = loudness * jnp.repeat(jnp.exp(steps), shape[axis_at] // shards_of).reshape((-1,) + (1,) * (len(shape) - 1 - axis_at))
    return loudness


def centred(stream_key, shape, spread, most, shards=(), kind=jnp.bfloat16):
    drawn = jax.random.normal(stream_key, shape, jnp.float32) * spread
    if len(shards) > 0:
        drawn = shard_levels(stream_key, shape, shards, -0.22, 0.18) * drawn
    return jnp.clip(drawn, min=-most, max=most).astype(kind)


def setup_inputs(seed: int = 0) -> dict:
    key_list = jax.random.split(jax.random.key(seed), 8)
    return {
        "teacher_hidden": draw_teacher_hidden(jax.random.fold_in(key_list[7], 71), 0),
        "teacher_gain": jnp.clip(1.0 + 0.1 * jax.random.normal(key_list[1], (DT,), jnp.float32), 0.5, 1.5),
        "projector": centred(key_list[2], (DT, DS), DT ** -0.5, 0.09375, ((0, 32), (1, 8))),
        "live": draw_live(jax.random.fold_in(key_list[7], 71), 0),
        "placement": draw_placement(jax.random.fold_in(key_list[7], 71), 0),
        "student_hidden": draw_student_hidden(jax.random.fold_in(key_list[7], 71), 0),
        "student_gain": jnp.clip(1.0 + 0.1 * jax.random.normal(key_list[6], (DS,), jnp.float32), 0.5, 1.5),
    }


EPSILON = 1e-06

def teacher_block(rows_block, teacher_gain, projector):
    values = rows_block.astype(jnp.float32)
    inverse_rms = lax.rsqrt(lax.optimization_barrier(jnp.mean(values * values, axis=-1, keepdims=True)) + EPSILON)
    normed = (values * inverse_rms * teacher_gain).astype(jnp.bfloat16)
    return jnp.dot(normed, projector, preferred_element_type=jnp.float32).astype(jnp.bfloat16)

def arrival(live, placement):
    classes = N_GROUP * N_MP
    extent = N_DP * TOK_DEV
    live_rows = live.reshape(N_GROUP, N_DP, N_MP, TOK_DEV).transpose(0, 2, 1, 3).reshape(classes, extent)
    shard_ids = placement.reshape(N_GROUP, N_DP, N_MP, TOK_DEV).transpose(0, 2, 1, 3).reshape(classes, extent)
    matches = ((shard_ids[:, :, None] == jnp.arange(N_DP, dtype=jnp.int32)[None, None, :]) & (live_rows[:, :, None] == 1)).astype(jnp.int32)
    earlier = jnp.cumsum(matches, axis=1, dtype=jnp.int32) - matches
    arrival_slot = lax.optimization_barrier(jnp.sum(earlier * matches, axis=-1, dtype=jnp.int32))
    group_class = jnp.arange(classes, dtype=jnp.int32)[:, None]
    destination = ((group_class // N_MP * N_DP + shard_ids) * N_MP + group_class % N_MP) * TOK_DEV + arrival_slot
    destination = jnp.where(live_rows == 1, destination, TOKENS).astype(jnp.int32)
    return destination.reshape(N_GROUP, N_MP, N_DP, TOK_DEV).transpose(0, 2, 1, 3).reshape(TOKENS)

def student_block(hidden_rows, target, filled, student_gain):
    values = hidden_rows.astype(jnp.float32)
    inverse_rms = lax.rsqrt(lax.optimization_barrier(jnp.mean(values * values, axis=-1, keepdims=True)) + EPSILON)
    normal = values * inverse_rms
    mismatch = (normal * student_gain - target.astype(jnp.float32)) * filled[:, None]
    weighted = mismatch * student_gain
    gradient = inverse_rms * (weighted - normal * lax.optimization_barrier(jnp.mean(weighted * normal, axis=-1, keepdims=True)))
    return (gradient.astype(jnp.bfloat16), lax.optimization_barrier(jnp.sum(mismatch * normal, axis=0)), jnp.sum(mismatch * mismatch))

def reference(teacher_hidden, teacher_gain, projector, live, placement, student_hidden, student_gain):
    blocks = teacher_hidden.reshape(TOKENS // TOK_DEV, TOK_DEV, DT)
    projected = lax.map(lambda rows_block: teacher_block(rows_block, teacher_gain, projector), blocks).reshape(TOKENS, DS)
    destination = arrival(live, placement)
    target = jnp.zeros((TOKENS, DS), jnp.bfloat16).at[destination].set(projected, mode='drop')
    filled = jnp.zeros((TOKENS,), jnp.float32).at[destination].set(1.0, mode='drop')
    count = jnp.sum(filled)
    pieces = (student_hidden.reshape(-1, TOK_DEV, DS), target.reshape(-1, TOK_DEV, DS), filled.reshape(-1, TOK_DEV))
    gradients, gain_terms, squares = lax.map(lambda triple: student_block(triple[0], triple[1], triple[2], student_gain), pieces)
    grad_gain = lax.optimization_barrier(jnp.sum(gain_terms, axis=0)) / count
    mean_loss = jnp.sum(squares) / (2.0 * count * DS)
    return (gradients.reshape(TOKENS, DS), grad_gain, mean_loss)
```

```python
import functools

import jax
import jax.numpy as jnp
from jax import lax
from jax.experimental import pallas as pl
from jax.experimental.pallas import tpu as pltpu
from jax.sharding import PartitionSpec as P

EPSILON = 1e-06
RING = 4
MIB = 1024 * 1024
EMPTY = 1e30
EMPTY_FROM = 1e20


def norm_kernel(moved_ref, slot_ref, gain_ref, top_ref, low_ref, packed):
    parts, rows, features = moved_ref.shape
    order = lax.broadcasted_iota(jnp.int32, (rows, rows), 0)
    packer = (order == slot_ref[...]).astype(jnp.bfloat16)
    total = jnp.zeros((rows, 1), jnp.float32)
    for part in range(parts):
        values = jnp.dot(packer, moved_ref[part], preferred_element_type=jnp.float32)
        packed[part] = values
        total += jnp.sum(values * values, axis=1, keepdims=True)
    inverse_rms = lax.rsqrt(total * (1.0 / (parts * features)) + EPSILON)
    half = rows // 2
    taken = jnp.sum(packer.astype(jnp.float32), axis=1, keepdims=True)
    first_column = lax.broadcasted_iota(jnp.int32, (rows, features), 1) == 0
    for part in range(parts):
        columns = slice(part * features, (part + 1) * features)
        normed = packed[part] * inverse_rms * gain_ref[:, columns]
        if part == 0:
            normed = jnp.where(first_column & (taken == 0.0), EMPTY, normed)
        normed = normed.astype(jnp.bfloat16)
        top_ref[:, columns] = normed[:half]
        low_ref[:, columns] = normed[half:]


def norm_rows(moved, slot, teacher_gain):
    parts, rows, features = moved.shape
    half = jax.ShapeDtypeStruct((rows // 2, parts * features), jnp.bfloat16)
    return pl.pallas_call(
        norm_kernel,
        out_shape=(half, half),
        scratch_shapes=[pltpu.VMEM((parts, rows, features), jnp.float32)],
        compiler_params=pltpu.CompilerParams(vmem_limit_bytes=16 * MIB),
        cost_estimate=pl.CostEstimate(
            flops=2 * rows * rows * parts * features,
            bytes_accessed=4 * rows * parts * features,
            transcendentals=rows,
        ),
    )(moved, slot[None, :], teacher_gain[None, :])


def product_kernel(shards, count, place_ref, *refs):
    sources, weight_sources = refs[:count], refs[count : count + 2]
    out_ref, rows_buffer, weights, sums, row_sems, weight_sems = refs[count + 2 :]
    y_count, shares = weights.shape[1:3]
    steps = weight_sems.shape[1]
    spans = y_count // steps
    part = rows_buffer.shape[1] // steps
    height = sources[0].shape[0]
    row_copies = [
        pltpu.make_async_copy(source, rows_buffer.at[pl.ds(i * height, height)], row_sems.at[i])
        for i, source in enumerate(sources)
    ]
    weight_copies = [
        [
            pltpu.make_async_copy(
                source.at[pl.ds(step * spans, spans)],
                weights.at[side, pl.ds(step * spans, spans)],
                weight_sems.at[side, step],
            )
            for step in range(steps)
        ]
        for side, source in enumerate(weight_sources)
    ]
    for copy in row_copies:
        copy.start()
    for step in range(steps):
        for side in range(2):
            weight_copies[side][step].start()
    for copy in row_copies:
        copy.wait()

    core = place_ref[0]
    for step in range(steps):
        rows = rows_buffer[:, step * part : (step + 1) * part]
        for side in range(2):
            weight_copies[side][step].wait()
            tiles = []
            for span in range(step * spans, (step + 1) * spans):
                for pair in range(shares // 2):
                    halves = weights[side, span, 2 * pair : 2 * pair + 2]
                    tiles.append(halves.reshape(-1, halves.shape[-1]))
            partial = lax.dot_general(
                rows,
                jnp.concatenate(tiles, axis=1),
                (((1,), (1,)), ((), ())),
                preferred_element_type=jnp.float32,
            )
            if step == 0:
                sums[side] = partial
            else:
                sums[side] += partial

    total_rows, width = sums.shape[1:]
    depth = total_rows // shards
    to = lax.broadcasted_iota(jnp.int32, (total_rows, total_rows), 0)
    source = lax.broadcasted_iota(jnp.int32, (total_rows, total_rows), 1)
    turn = (source == (to % depth) * shards + to // depth).astype(jnp.bfloat16)
    empty = rows_buffer[:, :128].astype(jnp.float32)[:, 0:1] > EMPTY_FROM

    def turned(side):
        kept = jnp.where(empty, EMPTY, sums[side]).astype(jnp.bfloat16)
        return jnp.dot(turn, kept, preferred_element_type=jnp.float32).astype(jnp.bfloat16)

    mine = turned(0)
    other = turned(1)

    @pl.when(core == 0)
    def _():
        out_ref[:, :width] = mine
        out_ref[:, width:] = other

    @pl.when(core != 0)
    def _():
        out_ref[:, :width] = other
        out_ref[:, width:] = mine


def product(place, pieces, mine, other, shards):
    y_count, shares, half, tile = mine.shape
    width = 2 * half
    depth = y_count * (shares // 2) * tile
    count = len(pieces)
    total_rows = pieces[0].shape[0] * count
    steps = 4
    return pl.pallas_call(
        functools.partial(product_kernel, shards, count),
        out_shape=jax.ShapeDtypeStruct((total_rows, 2 * width), jnp.bfloat16),
        in_specs=[pl.BlockSpec(memory_space=pltpu.SMEM)]
        + [pl.BlockSpec(memory_space=pl.ANY)] * (count + 2),
        out_specs=pl.BlockSpec(memory_space=pltpu.VMEM),
        scratch_shapes=[
            pltpu.VMEM((total_rows, depth), jnp.bfloat16),
            pltpu.VMEM((2,) + mine.shape, jnp.bfloat16),
            pltpu.VMEM((2, total_rows, width), jnp.float32),
            pltpu.SemaphoreType.DMA((count,)),
            pltpu.SemaphoreType.DMA((2, steps)),
        ],
        compiler_params=pltpu.CompilerParams(vmem_limit_bytes=32 * MIB),
        cost_estimate=pl.CostEstimate(
            flops=4 * total_rows * depth * width,
            bytes_accessed=2 * depth * (total_rows + 2 * width),
            transcendentals=0,
        ),
    )(place, *pieces, mine, other)


def finish_kernel(
    mp_count, received_ref, hidden_ref, gain_ref, gradient_ref, message_ref, weighted_sum, gain_sum
):
    y_count, x_count, deep, quarter = received_ref.shape
    rows, width = hidden_ref.shape
    capacity = deep // x_count
    spans = [slice(x * quarter, (x + 1) * quarter) for x in range(x_count)]
    total = jnp.zeros((rows, 1), jnp.float32)
    for span in spans:
        values = hidden_ref[:, span].astype(jnp.float32)
        total += jnp.sum(values * values, axis=1, keepdims=True)
    inverse_rms = lax.rsqrt(total * (1.0 / width) + EPSILON)
    to = lax.broadcasted_iota(jnp.int32, (rows, rows), 0)
    source = lax.broadcasted_iota(jnp.int32, (rows, rows), 1)

    def rank_of(row, x):
        y, j, rank = row // deep, (row // capacity) % x_count, row % capacity
        return (y * x_count + (x - j + x_count) % x_count) * capacity + rank

    row_terms = jnp.zeros((rows, 1), jnp.float32)
    squares = jnp.zeros((rows, 1), jnp.float32)
    tally = None
    for x, span in enumerate(spans):
        block = received_ref[:, x].reshape(y_count * deep, quarter)
        live = jnp.where(block[:, 0:1].astype(jnp.float32) < EMPTY_FROM, 1.0, 0.0)
        live = jnp.broadcast_to(live, (rows, rows))
        if tally is None:
            tally = jnp.sum(live, axis=0, keepdims=True)[:, 0:1]
            filled = (
                lax.broadcasted_iota(jnp.int32, (rows, 1), 0).astype(jnp.float32) < tally
            ).astype(jnp.float32)
        before = (rank_of(source, x) < rank_of(to, x)).astype(jnp.bfloat16)
        slot = jnp.dot(before, live.astype(jnp.bfloat16), preferred_element_type=jnp.float32)
        chooser = jnp.where(slot == source.astype(jnp.float32), live, 0.0).astype(jnp.bfloat16)
        target = lax.dot_general(
            chooser, block, (((0,), (0,)), ((), ())), preferred_element_type=jnp.float32
        )
        gain = gain_ref[:, span]
        normal = hidden_ref[:, span].astype(jnp.float32) * inverse_rms
        mismatch = (normal * gain - target) * filled
        weighted = mismatch * gain
        weighted_sum[:, span] = weighted
        row_terms += jnp.sum(weighted * normal, axis=1, keepdims=True)
        squares += jnp.sum(mismatch * mismatch, axis=1, keepdims=True)
        gain_sum[:, span] = jnp.sum(mismatch * normal, axis=0, keepdims=True)
    row_mean = row_terms * (1.0 / width)
    for span in spans:
        normal = hidden_ref[:, span].astype(jnp.float32) * inverse_rms
        gradient_ref[:, span] = (
            inverse_rms * (weighted_sum[:, span] - normal * row_mean)
        ).astype(jnp.bfloat16)
    share = width // mp_count
    square_sum = jnp.sum(squares, axis=0, keepdims=True)
    lane = lax.broadcasted_iota(jnp.int32, (1, message_ref.shape[2] - share), 1)
    tail = jnp.where(lane == 0, square_sum, jnp.where(lane == 1, tally, 0.0))
    for m in range(mp_count):
        message_ref[m, :, :share] = gain_sum[:, m * share : (m + 1) * share]
        message_ref[m, :, share:] = tail


def finish(received, hidden, gains, mp_count):
    rows, width = hidden.shape
    share = width // mp_count
    in_vmem = pl.BlockSpec(memory_space=pltpu.VMEM)
    return pl.pallas_call(
        functools.partial(finish_kernel, mp_count),
        out_shape=(
            jax.ShapeDtypeStruct((rows, width), jnp.bfloat16),
            jax.ShapeDtypeStruct((mp_count, 1, share + 64), jnp.float32),
        ),
        in_specs=[in_vmem] * 3,
        out_specs=(in_vmem, in_vmem),
        scratch_shapes=[
            pltpu.VMEM((rows, width), jnp.float32),
            pltpu.VMEM((1, width), jnp.float32),
        ],
        compiler_params=pltpu.CompilerParams(vmem_limit_bytes=16 * MIB),
        cost_estimate=pl.CostEstimate(
            flops=2 * rows * rows * width, bytes_accessed=6 * rows * width, transcendentals=rows
        ),
    )(received, hidden, gains[None, :])


def ring_gather(top, low, x_count, dp_count):
    forward = [(d, d - d % x_count + (d + 1) % x_count) for d in range(dp_count)]
    backward = [(d, d - d % x_count + (d - 1) % x_count) for d in range(dp_count)]
    left_top = lax.ppermute(top, "dp", forward)
    right_low = lax.ppermute(low, "dp", backward)
    left_low = lax.ppermute(low, "dp", forward)
    right_top = lax.ppermute(top, "dp", backward)
    far_top = lax.ppermute(left_top, "dp", forward)
    far_low = lax.ppermute(right_low, "dp", backward)
    return [top, low, left_top, left_low, far_top, far_low, right_top, right_low]


def projector_columns(projector, student_gain, mp_count, x_count, y_count):
    core = lax.axis_index("group")
    dp_count = x_count * y_count
    columns = projector.T
    half, tile = columns.shape[0] // 2, columns.shape[1]
    share = lax.dynamic_slice_in_dim(columns, core * half, half, 0)
    moves = []
    for c in range(2):
        for d in range(dp_count):
            for z in range(mp_count):
                source = (c * dp_count + d) * mp_count + z
                y, x = divmod(d, x_count)
                to_d = y * x_count + z // 2
                moves.append((source, ((z % 2) * dp_count + to_d) * mp_count + 2 * x + c))
    piece = lax.ppermute(share, ("group", "dp", "mp"), moves)
    high = lax.reduce_precision(student_gain, 8, 7)
    middle = lax.reduce_precision(student_gain - high, 8, 7)
    low = student_gain - high - middle
    width = student_gain.shape[0]
    extra = 16
    parts = jnp.concatenate(
        [high, middle, low, jnp.zeros((extra * tile - 3 * width,), jnp.float32)]
    ).astype(jnp.bfloat16)
    message = jnp.concatenate([piece, parts.reshape(extra, tile)], axis=0)
    spread = lax.all_to_all(
        jnp.broadcast_to(message[None], (mp_count,) + message.shape), "mp", 0, 0, tiled=True
    )
    parts = spread[:, half:].reshape(mp_count, extra * tile).astype(jnp.float32)
    gains = parts[:, :width] + parts[:, width : 2 * width] + parts[:, 2 * width : 3 * width]
    tiles = spread[:, :half].reshape(mp_count * half, tile)
    y_groups = [[y * x_count + x for y in range(y_count)] for x in range(x_count)]
    mine = lax.all_gather(tiles, "dp", axis=0, axis_index_groups=y_groups, tiled=True)
    return mine.reshape(y_count, mp_count, half, tile), gains.reshape(mp_count * width)


def local(teacher_hidden, teacher_gain, projector, live, placement, student_hidden, student_gain):
    dp_count = lax.axis_size("dp")
    mp_count = lax.axis_size("mp")
    group_count = lax.axis_size("group")
    x_count = RING
    y_count = dp_count // x_count
    column = lax.axis_index("mp")
    core = lax.axis_index("group")
    slot_count = student_hidden.shape[0]
    capacity = slot_count // dp_count
    share_width = student_gain.shape[0]
    width = share_width * mp_count

    features = teacher_hidden.shape[1]
    blocks = teacher_hidden.reshape(mp_count, slot_count, features)
    moved = lax.all_to_all(blocks, "mp", 0, 0, tiled=True)
    mine, gains = projector_columns(projector, student_gain, mp_count, x_count, y_count)

    own_live = lax.dynamic_index_in_dim(live.reshape(mp_count, slot_count), column, 0, keepdims=False)
    own_shards = lax.dynamic_index_in_dim(placement.reshape(mp_count, slot_count), column, 0, keepdims=False)
    order = jnp.arange(slot_count, dtype=jnp.int32)
    same = (
        (own_shards[:, None] == own_shards[None, :])
        & (own_live[:, None] == 1)
        & (order[:, None] < order[None, :])
    )
    rank = jnp.sum(same.astype(jnp.int32), axis=0)
    slot = jnp.where(own_live == 1, rank * dp_count + own_shards, -1)

    top, low = norm_rows(moved, slot, teacher_gain)
    pieces = ring_gather(top, low, x_count, dp_count)
    mine, pieces[2], pieces[3], pieces[6], pieces[7] = lax.optimization_barrier(
        (mine, pieces[2], pieces[3], pieces[6], pieces[7])
    )
    other = lax.ppermute(mine, "group", [(0, 1), (1, 0)])

    buffer = product(core.astype(jnp.int32).reshape(1), pieces, mine, other, dp_count)
    quarter = buffer.shape[1]
    deep = x_count * capacity
    received = lax.all_to_all(
        buffer.reshape(dp_count, deep, quarter), "dp", 0, 0, tiled=True
    ).reshape(y_count, x_count, deep, quarter)
    gradient, message = finish(received, student_hidden, gains, mp_count)

    over_mp = jnp.sum(lax.all_to_all(message, "mp", 0, 0, tiled=True), axis=(0, 1))
    peers = group_count * dp_count
    totals = jnp.sum(
        lax.all_to_all(
            jnp.broadcast_to(over_mp[None, :], (peers, over_mp.shape[0])), ("group", "dp"), 0, 0, tiled=True
        ),
        axis=0,
    )
    square_sum = totals[share_width]
    tally_sum = totals[share_width + 1]
    grad_gain = totals[:share_width] / tally_sum
    mean_loss = square_sum / (2.0 * tally_sum * width)
    return (gradient, grad_gain, mean_loss)


def solution(mesh):
    placed = (
        P(("group", "dp"), "mp"),
        P(),
        P("dp", "mp"),
        P(("group", "dp")),
        P(("group", "dp")),
        P(("group", "dp", "mp"), None),
        P("mp"),
    )
    return jax.shard_map(
        local,
        mesh=mesh,
        in_specs=placed,
        out_specs=(P(("group", "dp", "mp"), None), P("mp"), P()),
        check_vma=False,
    )
```

```python
import functools

import jax
import jax.numpy as jnp
from jax import lax
from jax.experimental import pallas as pl
from jax.experimental.pallas import tpu as pltpu
from jax.sharding import PartitionSpec as P

EPSILON = 1e-06
RING = 4
MIB = 1024 * 1024
EMPTY = 1e30
EMPTY_FROM = 1e20


def norm_kernel(moved_ref, slot_ref, gain_ref, top_ref, low_ref, packed):
    parts, rows, features = moved_ref.shape
    order = lax.broadcasted_iota(jnp.int32, (rows, rows), 0)
    packer = (order == slot_ref[...]).astype(jnp.bfloat16)
    total = jnp.zeros((rows, 1), jnp.float32)
    for part in range(parts):
        values = jnp.dot(packer, moved_ref[part], preferred_element_type=jnp.float32)
        packed[part] = values
        total += jnp.sum(values * values, axis=1, keepdims=True)
    inverse_rms = lax.rsqrt(total * (1.0 / (parts * features)) + EPSILON)
    half = rows // 2
    taken = jnp.sum(packer.astype(jnp.float32), axis=1, keepdims=True)
    first_column = lax.broadcasted_iota(jnp.int32, (rows, features), 1) == 0
    for part in range(parts):
        columns = slice(part * features, (part + 1) * features)
        normed = packed[part] * inverse_rms * gain_ref[:, columns]
        if part == 0:
            normed = jnp.where(first_column & (taken == 0.0), EMPTY, normed)
        normed = normed.astype(jnp.bfloat16)
        top_ref[:, columns] = normed[:half]
        low_ref[:, columns] = normed[half:]


def norm_rows(moved, slot, teacher_gain):
    parts, rows, features = moved.shape
    half = jax.ShapeDtypeStruct((rows // 2, parts * features), jnp.bfloat16)
    return pl.pallas_call(
        norm_kernel,
        out_shape=(half, half),
        scratch_shapes=[pltpu.VMEM((parts, rows, features), jnp.float32)],
        compiler_params=pltpu.CompilerParams(vmem_limit_bytes=16 * MIB),
        cost_estimate=pl.CostEstimate(
            flops=2 * rows * rows * parts * features,
            bytes_accessed=4 * rows * parts * features,
            transcendentals=rows,
        ),
    )(moved, slot[None, :], teacher_gain[None, :])


def block_product(sources, weight_source, rows_buffer, weights, total, row_sems, weight_sems):
    steps = weight_sems.shape[0]
    y_count, shares, half, tile = weights.shape
    spans = y_count // steps
    part = rows_buffer.shape[1] // steps
    height = sources[0].shape[0]
    copies = []
    for step in range(steps):
        features = pl.ds(step * part, part)
        chunk = [
            pltpu.make_async_copy(
                source.at[:, features],
                rows_buffer.at[pl.ds(i * height, height), features],
                row_sems.at[i, step],
            )
            for i, source in enumerate(sources)
        ]
        blocks = pl.ds(step * spans, spans)
        chunk.append(
            pltpu.make_async_copy(weight_source.at[blocks], weights.at[blocks], weight_sems.at[step])
        )
        copies.append(chunk)
    for chunk in copies:
        for copy in chunk:
            copy.start()
    for step in range(steps):
        for copy in copies[step]:
            copy.wait()
        tiles = [
            weights[span, 2 * pair : 2 * pair + 2].reshape(2 * half, tile)
            for span in range(step * spans, (step + 1) * spans)
            for pair in range(shares // 2)
        ]
        partial = lax.dot_general(
            rows_buffer[:, step * part : (step + 1) * part],
            jnp.concatenate(tiles, axis=1),
            (((1,), (1,)), ((), ())),
            preferred_element_type=jnp.float32,
        )
        if step == 0:
            total[...] = partial
        else:
            total[...] += partial


def turned(shards, total, rows_buffer):
    rows = total.shape[0]
    depth = rows // shards
    to = lax.broadcasted_iota(jnp.int32, (rows, rows), 0)
    source = lax.broadcasted_iota(jnp.int32, (rows, rows), 1)
    turn = (source == (to % depth) * shards + to // depth).astype(jnp.bfloat16)
    empty = rows_buffer[:, :128].astype(jnp.float32)[:, 0:1] > EMPTY_FROM
    kept = jnp.where(empty, EMPTY, total[...]).astype(jnp.bfloat16)
    return jnp.dot(turn, kept, preferred_element_type=jnp.float32).astype(jnp.bfloat16)


def first_kernel(shards, count, *refs):
    out_ref, rows_buffer, weights, total, row_sems, weight_sems = refs[count + 1 :]
    block_product(refs[:count], refs[count], rows_buffer, weights, total, row_sems, weight_sems)
    out_ref[...] = turned(shards, total, rows_buffer)


def second_kernel(shards, count, core_ref, first_ref, *refs):
    out_ref, rows_buffer, weights, total, row_sems, weight_sems = refs[count + 1 :]
    block_product(refs[:count], refs[count], rows_buffer, weights, total, row_sems, weight_sems)
    width = total.shape[1]
    mine = first_ref[...]
    other = turned(shards, total, rows_buffer)

    @pl.when(core_ref[0] == 0)
    def _():
        out_ref[:, :width] = mine
        out_ref[:, width:] = other

    @pl.when(core_ref[0] != 0)
    def _():
        out_ref[:, :width] = other
        out_ref[:, width:] = mine


def product(pieces, weights, shards, core=None, first=None):
    y_count, shares, half, tile = weights.shape
    width = 2 * half
    depth = y_count * (shares // 2) * tile
    count = len(pieces)
    total_rows = pieces[0].shape[0] * count
    steps = 4
    joined = first is not None
    in_vmem = pl.BlockSpec(memory_space=pltpu.VMEM)
    head = [pl.BlockSpec(memory_space=pltpu.SMEM), in_vmem] if joined else []
    kernel = second_kernel if joined else first_kernel
    return pl.pallas_call(
        functools.partial(kernel, shards, count),
        out_shape=jax.ShapeDtypeStruct(
            (total_rows, 2 * width if joined else width), jnp.bfloat16
        ),
        in_specs=head + [pl.BlockSpec(memory_space=pl.ANY)] * (count + 1),
        out_specs=in_vmem,
        scratch_shapes=[
            pltpu.VMEM((total_rows, depth), jnp.bfloat16),
            pltpu.VMEM(weights.shape, jnp.bfloat16),
            pltpu.VMEM((total_rows, width), jnp.float32),
            pltpu.SemaphoreType.DMA((count, steps)),
            pltpu.SemaphoreType.DMA((steps,)),
        ],
        compiler_params=pltpu.CompilerParams(vmem_limit_bytes=56 * MIB),
        cost_estimate=pl.CostEstimate(
            flops=2 * total_rows * depth * width,
            bytes_accessed=2 * depth * (total_rows + width),
            transcendentals=0,
        ),
    )(*((core, first) if joined else ()), *pieces, weights)


def finish_kernel(
    mp_count, received_ref, hidden_ref, gain_ref, gradient_ref, message_ref, weighted_sum, gain_sum
):
    y_count, x_count, deep, quarter = received_ref.shape
    rows, width = hidden_ref.shape
    capacity = deep // x_count
    spans = [slice(x * quarter, (x + 1) * quarter) for x in range(x_count)]
    total = jnp.zeros((rows, 1), jnp.float32)
    for span in spans:
        values = hidden_ref[:, span].astype(jnp.float32)
        total += jnp.sum(values * values, axis=1, keepdims=True)
    inverse_rms = lax.rsqrt(total * (1.0 / width) + EPSILON)
    to = lax.broadcasted_iota(jnp.int32, (rows, rows), 0)
    source = lax.broadcasted_iota(jnp.int32, (rows, rows), 1)

    def rank_of(row, x):
        y, j, rank = row // deep, (row // capacity) % x_count, row % capacity
        return (y * x_count + (x - j + x_count) % x_count) * capacity + rank

    row_terms = jnp.zeros((rows, 1), jnp.float32)
    squares = jnp.zeros((rows, 1), jnp.float32)
    tally = None
    for x, span in enumerate(spans):
        block = received_ref[:, x].reshape(y_count * deep, quarter)
        live = jnp.where(block[:, 0:1].astype(jnp.float32) < EMPTY_FROM, 1.0, 0.0)
        live = jnp.broadcast_to(live, (rows, rows))
        if tally is None:
            tally = jnp.sum(live, axis=0, keepdims=True)[:, 0:1]
            filled = (
                lax.broadcasted_iota(jnp.int32, (rows, 1), 0).astype(jnp.float32) < tally
            ).astype(jnp.float32)
        before = (rank_of(source, x) < rank_of(to, x)).astype(jnp.bfloat16)
        slot = jnp.dot(before, live.astype(jnp.bfloat16), preferred_element_type=jnp.float32)
        chooser = jnp.where(slot == source.astype(jnp.float32), live, 0.0).astype(jnp.bfloat16)
        target = lax.dot_general(
            chooser, block, (((0,), (0,)), ((), ())), preferred_element_type=jnp.float32
        )
        gain = gain_ref[:, span]
        normal = hidden_ref[:, span].astype(jnp.float32) * inverse_rms
        mismatch = (normal * gain - target) * filled
        weighted = mismatch * gain
        weighted_sum[:, span] = weighted
        row_terms += jnp.sum(weighted * normal, axis=1, keepdims=True)
        squares += jnp.sum(mismatch * mismatch, axis=1, keepdims=True)
        gain_sum[:, span] = jnp.sum(mismatch * normal, axis=0, keepdims=True)
    row_mean = row_terms * (1.0 / width)
    for span in spans:
        normal = hidden_ref[:, span].astype(jnp.float32) * inverse_rms
        gradient_ref[:, span] = (
            inverse_rms * (weighted_sum[:, span] - normal * row_mean)
        ).astype(jnp.bfloat16)
    share = width // mp_count
    square_sum = jnp.sum(squares, axis=0, keepdims=True)
    lane = lax.broadcasted_iota(jnp.int32, (1, message_ref.shape[2] - share), 1)
    tail = jnp.where(lane == 0, square_sum, jnp.where(lane == 1, tally, 0.0))
    for m in range(mp_count):
        message_ref[m, :, :share] = gain_sum[:, m * share : (m + 1) * share]
        message_ref[m, :, share:] = tail


def finish(received, hidden, gains, mp_count):
    rows, width = hidden.shape
    share = width // mp_count
    in_vmem = pl.BlockSpec(memory_space=pltpu.VMEM)
    return pl.pallas_call(
        functools.partial(finish_kernel, mp_count),
        out_shape=(
            jax.ShapeDtypeStruct((rows, width), jnp.bfloat16),
            jax.ShapeDtypeStruct((mp_count, 1, share + 64), jnp.float32),
        ),
        in_specs=[in_vmem] * 3,
        out_specs=(in_vmem, in_vmem),
        scratch_shapes=[
            pltpu.VMEM((rows, width), jnp.float32),
            pltpu.VMEM((1, width), jnp.float32),
        ],
        compiler_params=pltpu.CompilerParams(vmem_limit_bytes=16 * MIB),
        cost_estimate=pl.CostEstimate(
            flops=2 * rows * rows * width, bytes_accessed=6 * rows * width, transcendentals=rows
        ),
    )(received, hidden, gains[None, :])


def ring_gather(top, low, x_count, dp_count):
    forward = [(d, d - d % x_count + (d + 1) % x_count) for d in range(dp_count)]
    backward = [(d, d - d % x_count + (d - 1) % x_count) for d in range(dp_count)]
    left_top = lax.ppermute(top, "dp", forward)
    right_low = lax.ppermute(low, "dp", backward)
    left_low = lax.ppermute(low, "dp", forward)
    right_top = lax.ppermute(top, "dp", backward)
    far_top = lax.ppermute(left_top, "dp", forward)
    far_low = lax.ppermute(right_low, "dp", backward)
    return [top, low, left_top, left_low, far_top, far_low, right_top, right_low]


def projector_columns(projector, student_gain, mp_count, x_count, y_count):
    core = lax.axis_index("group")
    dp_count = x_count * y_count
    columns = projector.T
    half, tile = columns.shape[0] // 2, columns.shape[1]
    share = lax.dynamic_slice_in_dim(columns, core * half, half, 0)
    moves = []
    for c in range(2):
        for d in range(dp_count):
            for z in range(mp_count):
                source = (c * dp_count + d) * mp_count + z
                y, x = divmod(d, x_count)
                to_d = y * x_count + z // 2
                moves.append((source, ((z % 2) * dp_count + to_d) * mp_count + 2 * x + c))
    piece = lax.ppermute(share, ("group", "dp", "mp"), moves)
    high = lax.reduce_precision(student_gain, 8, 7)
    middle = lax.reduce_precision(student_gain - high, 8, 7)
    low = student_gain - high - middle
    width = student_gain.shape[0]
    extra = 16
    parts = jnp.concatenate(
        [high, middle, low, jnp.zeros((extra * tile - 3 * width,), jnp.float32)]
    ).astype(jnp.bfloat16)
    message = jnp.concatenate([piece, parts.reshape(extra, tile)], axis=0)
    spread = lax.all_to_all(
        jnp.broadcast_to(message[None], (mp_count,) + message.shape), "mp", 0, 0, tiled=True
    )
    parts = spread[:, half:].reshape(mp_count, extra * tile).astype(jnp.float32)
    gains = parts[:, :width] + parts[:, width : 2 * width] + parts[:, 2 * width : 3 * width]
    tiles = spread[:, :half].reshape(mp_count * half, tile)
    y_groups = [[y * x_count + x for y in range(y_count)] for x in range(x_count)]
    mine = lax.all_gather(tiles, "dp", axis=0, axis_index_groups=y_groups, tiled=True)
    return mine.reshape(y_count, mp_count, half, tile), gains.reshape(mp_count * width)


def local(teacher_hidden, teacher_gain, projector, live, placement, student_hidden, student_gain):
    dp_count = lax.axis_size("dp")
    mp_count = lax.axis_size("mp")
    group_count = lax.axis_size("group")
    x_count = RING
    y_count = dp_count // x_count
    column = lax.axis_index("mp")
    core = lax.axis_index("group")
    slot_count = student_hidden.shape[0]
    capacity = slot_count // dp_count
    share_width = student_gain.shape[0]
    width = share_width * mp_count

    features = teacher_hidden.shape[1]
    blocks = teacher_hidden.reshape(mp_count, slot_count, features)
    moved = lax.all_to_all(blocks, "mp", 0, 0, tiled=True)
    mine, gains = projector_columns(projector, student_gain, mp_count, x_count, y_count)

    own_live = lax.dynamic_index_in_dim(live.reshape(mp_count, slot_count), column, 0, keepdims=False)
    own_shards = lax.dynamic_index_in_dim(placement.reshape(mp_count, slot_count), column, 0, keepdims=False)
    order = jnp.arange(slot_count, dtype=jnp.int32)
    same = (
        (own_shards[:, None] == own_shards[None, :])
        & (own_live[:, None] == 1)
        & (order[:, None] < order[None, :])
    )
    rank = jnp.sum(same.astype(jnp.int32), axis=0)
    slot = jnp.where(own_live == 1, rank * dp_count + own_shards, -1)

    top, low = norm_rows(moved, slot, teacher_gain)
    pieces = ring_gather(top, low, x_count, dp_count)
    mine, pieces = lax.optimization_barrier((mine, pieces))
    other = lax.ppermute(mine, "group", [(0, 1), (1, 0)])
    first = product(pieces, mine, dp_count)
    buffer = product(pieces, other, dp_count, core.astype(jnp.int32).reshape(1), first)
    quarter = buffer.shape[1]
    deep = x_count * capacity
    received = lax.all_to_all(
        buffer.reshape(dp_count, deep, quarter), "dp", 0, 0, tiled=True
    ).reshape(y_count, x_count, deep, quarter)
    gradient, message = finish(received, student_hidden, gains, mp_count)

    over_mp = jnp.sum(lax.all_to_all(message, "mp", 0, 0, tiled=True), axis=(0, 1))
    peers = group_count * dp_count
    totals = jnp.sum(
        lax.all_to_all(
            jnp.broadcast_to(over_mp[None, :], (peers, over_mp.shape[0])), ("group", "dp"), 0, 0, tiled=True
        ),
        axis=0,
    )
    square_sum = totals[share_width]
    tally_sum = totals[share_width + 1]
    grad_gain = totals[:share_width] / tally_sum
    mean_loss = square_sum / (2.0 * tally_sum * width)
    return (gradient, grad_gain, mean_loss)


def solution(mesh):
    placed = (
        P(("group", "dp"), "mp"),
        P(),
        P("dp", "mp"),
        P(("group", "dp")),
        P(("group", "dp")),
        P(("group", "dp", "mp"), None),
        P("mp"),
    )
    return jax.shard_map(
        local,
        mesh=mesh,
        in_specs=placed,
        out_specs=(P(("group", "dp", "mp"), None), P("mp"), P()),
        check_vma=False,
    )
```

```python
import functools

import jax
import jax.numpy as jnp
from jax import lax
from jax.experimental import pallas as pl
from jax.experimental.pallas import tpu as pltpu
from jax.sharding import PartitionSpec as P

EPSILON = 1e-06
RING = 4
MIB = 1024 * 1024
SLOT_LANES = 128
EMPTY = 1e30
EMPTY_FROM = 1e20


def norm_kernel(moved_ref, slot_ref, gain_ref, out_ref):
    parts, rows, features = moved_ref.shape
    total = jnp.zeros((rows, 1), jnp.float32)
    for part in range(parts):
        values = moved_ref[part].astype(jnp.float32)
        total += jnp.sum(values * values, axis=1, keepdims=True)
    inverse_rms = lax.rsqrt(total * (1.0 / (parts * features)) + EPSILON)
    for part in range(parts):
        columns = slice(part * features, (part + 1) * features)
        values = moved_ref[part].astype(jnp.float32)
        out_ref[:, columns] = (values * inverse_rms * gain_ref[:, columns]).astype(jnp.bfloat16)
    slot = slot_ref[...].astype(jnp.float32)
    out_ref[:, parts * features :] = jnp.broadcast_to(slot, (rows, SLOT_LANES)).astype(jnp.bfloat16)


def norm_rows(moved, slot, teacher_gain):
    parts, rows, features = moved.shape
    return pl.pallas_call(
        norm_kernel,
        out_shape=jax.ShapeDtypeStruct((rows, parts * features + SLOT_LANES), jnp.bfloat16),
        compiler_params=pltpu.CompilerParams(vmem_limit_bytes=16 * MIB),
        cost_estimate=pl.CostEstimate(
            flops=4 * rows * parts * features,
            bytes_accessed=4 * rows * parts * features,
            transcendentals=rows,
        ),
    )(moved, slot[:, None], teacher_gain[None, :])


def block_product(
    sources, weight_source, rows_buffer, slots, weights, total, row_sems, slot_sems, weight_sems
):
    steps = weight_sems.shape[0]
    y_count, shares, half, tile = weights.shape
    spans = y_count // steps
    part = rows_buffer.shape[1] // steps
    height = sources[0].shape[0]
    copies = []
    for step in range(steps):
        features = pl.ds(step * part, part)
        chunk = [
            pltpu.make_async_copy(
                source.at[:, features],
                rows_buffer.at[pl.ds(i * height, height), features],
                row_sems.at[i, step],
            )
            for i, source in enumerate(sources)
        ]
        blocks = pl.ds(step * spans, spans)
        chunk.append(
            pltpu.make_async_copy(weight_source.at[blocks], weights.at[blocks], weight_sems.at[step])
        )
        copies.append(chunk)
    depth = rows_buffer.shape[1]
    copies[-1] += [
        pltpu.make_async_copy(
            source.at[:, pl.ds(depth, SLOT_LANES)],
            slots.at[pl.ds(i * height, height)],
            slot_sems.at[i],
        )
        for i, source in enumerate(sources)
    ]
    for chunk in copies:
        for copy in chunk:
            copy.start()
    for step in range(steps):
        for copy in copies[step]:
            copy.wait()
        tiles = [
            weights[span, 2 * pair : 2 * pair + 2].reshape(2 * half, tile)
            for span in range(step * spans, (step + 1) * spans)
            for pair in range(shares // 2)
        ]
        partial = lax.dot_general(
            rows_buffer[:, step * part : (step + 1) * part],
            jnp.concatenate(tiles, axis=1),
            (((1,), (1,)), ((), ())),
            preferred_element_type=jnp.float32,
        )
        if step == 0:
            total[...] = partial
        else:
            total[...] += partial


def turned(shards, total, slots):
    rows = total.shape[0]
    capacity = SLOT_LANES // shards
    block = SLOT_LANES
    source = lax.broadcasted_iota(jnp.int32, (rows, rows), 0)
    to = lax.broadcasted_iota(jnp.int32, (rows, rows), 1)
    depth = rows // shards
    wanted = (to % capacity) * shards + to // depth
    here = (to // capacity) % (depth // capacity) == source // block
    slot = slots[...].astype(jnp.float32)[:, 0:1]
    chosen = (here & (slot == wanted.astype(jnp.float32))).astype(jnp.bfloat16)

    def gathered(values):
        return lax.dot_general(
            chosen, values, (((0,), (0,)), ((), ())), preferred_element_type=jnp.float32
        )

    held = gathered(jnp.ones((rows, SLOT_LANES), jnp.bfloat16))[:, 0:1]
    placed = gathered(total[...].astype(jnp.bfloat16))
    return jnp.where(held > 0.5, placed, EMPTY).astype(jnp.bfloat16)


def first_kernel(shards, count, *refs):
    out_ref, rows_buffer, slots, weights, total, *sems = refs[count + 1 :]
    block_product(refs[:count], refs[count], rows_buffer, slots, weights, total, *sems)
    out_ref[...] = turned(shards, total, slots)


def second_kernel(shards, count, core_ref, first_ref, *refs):
    out_ref, rows_buffer, slots, weights, total, *sems = refs[count + 1 :]
    block_product(refs[:count], refs[count], rows_buffer, slots, weights, total, *sems)
    width = total.shape[1]
    mine = first_ref[...]
    other = turned(shards, total, slots)

    @pl.when(core_ref[0] == 0)
    def _():
        out_ref[:, :width] = mine
        out_ref[:, width:] = other

    @pl.when(core_ref[0] != 0)
    def _():
        out_ref[:, :width] = other
        out_ref[:, width:] = mine


def product(pieces, weights, shards, core=None, first=None):
    y_count, shares, half, tile = weights.shape
    width = 2 * half
    depth = y_count * (shares // 2) * tile
    count = len(pieces)
    total_rows = pieces[0].shape[0] * count
    steps = 4
    joined = first is not None
    in_vmem = pl.BlockSpec(memory_space=pltpu.VMEM)
    head = [pl.BlockSpec(memory_space=pltpu.SMEM), in_vmem] if joined else []
    kernel = second_kernel if joined else first_kernel
    return pl.pallas_call(
        functools.partial(kernel, shards, count),
        out_shape=jax.ShapeDtypeStruct(
            (total_rows, 2 * width if joined else width), jnp.bfloat16
        ),
        in_specs=head + [pl.BlockSpec(memory_space=pl.ANY)] * (count + 1),
        out_specs=in_vmem,
        scratch_shapes=[
            pltpu.VMEM((total_rows, depth), jnp.bfloat16),
            pltpu.VMEM((total_rows, SLOT_LANES), jnp.bfloat16),
            pltpu.VMEM(weights.shape, jnp.bfloat16),
            pltpu.VMEM((total_rows, width), jnp.float32),
            pltpu.SemaphoreType.DMA((count, steps)),
            pltpu.SemaphoreType.DMA((count,)),
            pltpu.SemaphoreType.DMA((steps,)),
        ],
        compiler_params=pltpu.CompilerParams(vmem_limit_bytes=56 * MIB),
        cost_estimate=pl.CostEstimate(
            flops=2 * total_rows * depth * width,
            bytes_accessed=2 * depth * (total_rows + width),
            transcendentals=0,
        ),
    )(*((core, first) if joined else ()), *pieces, weights)


def finish_kernel(
    mp_count, received_ref, hidden_ref, gain_ref, gradient_ref, message_ref, weighted_sum, gain_sum
):
    y_count, x_count, deep, quarter = received_ref.shape
    rows, width = hidden_ref.shape
    capacity = deep // x_count
    spans = [slice(x * quarter, (x + 1) * quarter) for x in range(x_count)]
    total = jnp.zeros((rows, 1), jnp.float32)
    for span in spans:
        values = hidden_ref[:, span].astype(jnp.float32)
        total += jnp.sum(values * values, axis=1, keepdims=True)
    inverse_rms = lax.rsqrt(total * (1.0 / width) + EPSILON)
    to = lax.broadcasted_iota(jnp.int32, (rows, rows), 0)
    source = lax.broadcasted_iota(jnp.int32, (rows, rows), 1)

    def rank_of(row, x):
        y, j, rank = row // deep, (row // capacity) % x_count, row % capacity
        return (y * x_count + (x - j + x_count) % x_count) * capacity + rank

    row_terms = jnp.zeros((rows, 1), jnp.float32)
    squares = jnp.zeros((rows, 1), jnp.float32)
    tally = None
    for x, span in enumerate(spans):
        block = received_ref[:, x].reshape(y_count * deep, quarter)
        live = jnp.where(block[:, 0:1].astype(jnp.float32) < EMPTY_FROM, 1.0, 0.0)
        live = jnp.broadcast_to(live, (rows, rows))
        if tally is None:
            tally = jnp.sum(live, axis=0, keepdims=True)[:, 0:1]
            filled = (
                lax.broadcasted_iota(jnp.int32, (rows, 1), 0).astype(jnp.float32) < tally
            ).astype(jnp.float32)
        before = (rank_of(source, x) < rank_of(to, x)).astype(jnp.bfloat16)
        slot = jnp.dot(before, live.astype(jnp.bfloat16), preferred_element_type=jnp.float32)
        chooser = jnp.where(slot == source.astype(jnp.float32), live, 0.0).astype(jnp.bfloat16)
        target = lax.dot_general(
            chooser, block, (((0,), (0,)), ((), ())), preferred_element_type=jnp.float32
        )
        gain = gain_ref[:, span]
        normal = hidden_ref[:, span].astype(jnp.float32) * inverse_rms
        mismatch = (normal * gain - target) * filled
        weighted = mismatch * gain
        weighted_sum[:, span] = weighted
        row_terms += jnp.sum(weighted * normal, axis=1, keepdims=True)
        squares += jnp.sum(mismatch * mismatch, axis=1, keepdims=True)
        gain_sum[:, span] = jnp.sum(mismatch * normal, axis=0, keepdims=True)
    row_mean = row_terms * (1.0 / width)
    for span in spans:
        normal = hidden_ref[:, span].astype(jnp.float32) * inverse_rms
        gradient_ref[:, span] = (
            inverse_rms * (weighted_sum[:, span] - normal * row_mean)
        ).astype(jnp.bfloat16)
    share = width // mp_count
    square_sum = jnp.sum(squares, axis=0, keepdims=True)
    lane = lax.broadcasted_iota(jnp.int32, (1, message_ref.shape[2] - share), 1)
    tail = jnp.where(lane == 0, square_sum, jnp.where(lane == 1, tally, 0.0))
    for m in range(mp_count):
        message_ref[m, :, :share] = gain_sum[:, m * share : (m + 1) * share]
        message_ref[m, :, share:] = tail


def finish(received, hidden, gains, mp_count):
    rows, width = hidden.shape
    share = width // mp_count
    in_vmem = pl.BlockSpec(memory_space=pltpu.VMEM)
    return pl.pallas_call(
        functools.partial(finish_kernel, mp_count),
        out_shape=(
            jax.ShapeDtypeStruct((rows, width), jnp.bfloat16),
            jax.ShapeDtypeStruct((mp_count, 1, share + 64), jnp.float32),
        ),
        in_specs=[in_vmem] * 3,
        out_specs=(in_vmem, in_vmem),
        scratch_shapes=[
            pltpu.VMEM((rows, width), jnp.float32),
            pltpu.VMEM((1, width), jnp.float32),
        ],
        compiler_params=pltpu.CompilerParams(vmem_limit_bytes=16 * MIB),
        cost_estimate=pl.CostEstimate(
            flops=2 * rows * rows * width, bytes_accessed=6 * rows * width, transcendentals=rows
        ),
    )(received, hidden, gains[None, :])


def ring_moves(x_count, dp_count):
    forward = [(d, d - d % x_count + (d + 1) % x_count) for d in range(dp_count)]
    backward = [(d, d - d % x_count + (d - 1) % x_count) for d in range(dp_count)]
    return forward, backward


def projector_columns(projector, student_gain, after, mp_count, x_count, y_count):
    core = lax.axis_index("group")
    dp_count = x_count * y_count
    columns = projector.T
    half, tile = columns.shape[0] // 2, columns.shape[1]
    share = lax.dynamic_slice_in_dim(columns, core * half, half, 0)
    moves = []
    for c in range(2):
        for d in range(dp_count):
            for z in range(mp_count):
                source = (c * dp_count + d) * mp_count + z
                y, x = divmod(d, x_count)
                to_d = y * x_count + z // 2
                moves.append((source, ((z % 2) * dp_count + to_d) * mp_count + 2 * x + c))
    piece = lax.ppermute(share, ("group", "dp", "mp"), moves)
    high = lax.reduce_precision(student_gain, 8, 7)
    middle = lax.reduce_precision(student_gain - high, 8, 7)
    low = student_gain - high - middle
    width = student_gain.shape[0]
    extra = 16
    parts = jnp.concatenate(
        [high, middle, low, jnp.zeros((extra * tile - 3 * width,), jnp.float32)]
    ).astype(jnp.bfloat16)
    message = jnp.concatenate([piece, parts.reshape(extra, tile)], axis=0)
    message, _ = lax.optimization_barrier((message, after))
    spread = lax.all_to_all(
        jnp.broadcast_to(message[None], (mp_count,) + message.shape), "mp", 0, 0, tiled=True
    )
    parts = spread[:, half:].reshape(mp_count, extra * tile).astype(jnp.float32)
    gains = parts[:, :width] + parts[:, width : 2 * width] + parts[:, 2 * width : 3 * width]
    tiles = spread[:, :half].reshape(mp_count * half, tile)
    y_groups = [[y * x_count + x for y in range(y_count)] for x in range(x_count)]
    mine = lax.all_gather(tiles, "dp", axis=0, axis_index_groups=y_groups, tiled=True)
    return mine.reshape(y_count, mp_count, half, tile), gains.reshape(mp_count * width), spread


def local(teacher_hidden, teacher_gain, projector, live, placement, student_hidden, student_gain):
    dp_count = lax.axis_size("dp")
    mp_count = lax.axis_size("mp")
    group_count = lax.axis_size("group")
    x_count = RING
    y_count = dp_count // x_count
    column = lax.axis_index("mp")
    core = lax.axis_index("group")
    slot_count = student_hidden.shape[0]
    capacity = slot_count // dp_count
    share_width = student_gain.shape[0]
    width = share_width * mp_count

    features = teacher_hidden.shape[1]
    blocks = teacher_hidden.reshape(mp_count, slot_count, features)
    half = slot_count // 2
    top_rows, low_rows = blocks[:, :half], blocks[:, half:]
    moved_top = lax.all_to_all(top_rows, "mp", 0, 0, tiled=True)
    mine, gains, spread = projector_columns(
        projector, student_gain, moved_top, mp_count, x_count, y_count
    )
    moved_top, low_rows, _ = lax.optimization_barrier((moved_top, low_rows, spread))
    moved_low = lax.all_to_all(low_rows, "mp", 0, 0, tiled=True)

    own_live = lax.dynamic_index_in_dim(live.reshape(mp_count, slot_count), column, 0, keepdims=False)
    own_shards = lax.dynamic_index_in_dim(placement.reshape(mp_count, slot_count), column, 0, keepdims=False)
    order = jnp.arange(slot_count, dtype=jnp.int32)
    same = (
        (own_shards[:, None] == own_shards[None, :])
        & (own_live[:, None] == 1)
        & (order[:, None] < order[None, :])
    )
    rank = jnp.sum(same.astype(jnp.int32), axis=0)
    slot = jnp.where(own_live == 1, rank * dp_count + own_shards, -1)

    top = norm_rows(moved_top, slot[:half], teacher_gain)
    forward, backward = ring_moves(x_count, dp_count)
    left_top = lax.ppermute(top, "dp", forward)
    right_top = lax.ppermute(top, "dp", backward)
    far_top = lax.ppermute(left_top, "dp", forward)
    moved_low, left_top, right_top = lax.optimization_barrier((moved_low, left_top, right_top))
    low = norm_rows(moved_low, slot[half:], teacher_gain)
    left_low = lax.ppermute(low, "dp", forward)
    right_low = lax.ppermute(low, "dp", backward)
    far_low = lax.ppermute(right_low, "dp", backward)
    pieces = [top, low, left_top, left_low, far_top, far_low, right_top, right_low]
    mine, pieces = lax.optimization_barrier((mine, pieces))
    other = lax.ppermute(mine, "group", [(0, 1), (1, 0)])
    first = product(pieces, mine, dp_count)
    buffer = product(pieces, other, dp_count, core.astype(jnp.int32).reshape(1), first)
    quarter = buffer.shape[1]
    deep = x_count * capacity
    received = lax.all_to_all(
        buffer.reshape(dp_count, deep, quarter), "dp", 0, 0, tiled=True
    ).reshape(y_count, x_count, deep, quarter)
    gradient, message = finish(received, student_hidden, gains, mp_count)

    over_mp = jnp.sum(lax.all_to_all(message, "mp", 0, 0, tiled=True), axis=(0, 1))
    peers = group_count * dp_count
    totals = jnp.sum(
        lax.all_to_all(
            jnp.broadcast_to(over_mp[None, :], (peers, over_mp.shape[0])), ("group", "dp"), 0, 0, tiled=True
        ),
        axis=0,
    )
    square_sum = totals[share_width]
    tally_sum = totals[share_width + 1]
    grad_gain = totals[:share_width] / tally_sum
    mean_loss = square_sum / (2.0 * tally_sum * width)
    return (gradient, grad_gain, mean_loss)


def solution(mesh):
    placed = (
        P(("group", "dp"), "mp"),
        P(),
        P("dp", "mp"),
        P(("group", "dp")),
        P(("group", "dp")),
        P(("group", "dp", "mp"), None),
        P("mp"),
    )
    return jax.shard_map(
        local,
        mesh=mesh,
        in_specs=placed,
        out_specs=(P(("group", "dp", "mp"), None), P("mp"), P()),
        check_vma=False,
    )
```

```python
import functools

import jax
import jax.numpy as jnp
from jax import lax
from jax.experimental import pallas as pl
from jax.experimental.pallas import tpu as pltpu
from jax.sharding import PartitionSpec as P

EPSILON = 1e-06
RING = 4
MIB = 1024 * 1024
EMPTY = 1e30
EMPTY_FROM = 1e20


def norm_kernel(moved_ref, slot_ref, gain_ref, top_ref, low_ref, packed):
    parts, rows, features = moved_ref.shape
    order = lax.broadcasted_iota(jnp.int32, (rows, rows), 0)
    packer = (order == slot_ref[...]).astype(jnp.bfloat16)
    total = jnp.zeros((rows, 1), jnp.float32)
    for part in range(parts):
        values = jnp.dot(packer, moved_ref[part], preferred_element_type=jnp.float32)
        packed[part] = values
        total += jnp.sum(values * values, axis=1, keepdims=True)
    inverse_rms = lax.rsqrt(total * (1.0 / (parts * features)) + EPSILON)
    half = rows // 2
    taken = jnp.sum(packer.astype(jnp.float32), axis=1, keepdims=True)
    first_column = lax.broadcasted_iota(jnp.int32, (rows, features), 1) == 0
    for part in range(parts):
        columns = slice(part * features, (part + 1) * features)
        normed = packed[part] * inverse_rms * gain_ref[:, columns]
        if part == 0:
            normed = jnp.where(first_column & (taken == 0.0), EMPTY, normed)
        normed = normed.astype(jnp.bfloat16)
        top_ref[:, columns] = normed[:half]
        low_ref[:, columns] = normed[half:]


def norm_rows(moved, slot, teacher_gain):
    parts, rows, features = moved.shape
    half = jax.ShapeDtypeStruct((rows // 2, parts * features), jnp.bfloat16)
    return pl.pallas_call(
        norm_kernel,
        out_shape=(half, half),
        scratch_shapes=[pltpu.VMEM((parts, rows, features), jnp.float32)],
        compiler_params=pltpu.CompilerParams(vmem_limit_bytes=16 * MIB),
        cost_estimate=pl.CostEstimate(
            flops=2 * rows * rows * parts * features,
            bytes_accessed=4 * rows * parts * features,
            transcendentals=rows,
        ),
    )(moved, slot[None, :], teacher_gain[None, :])


def block_product(start, sources, weight_source, rows_buffer, weights, total, row_sems, weight_sems):
    steps = weight_sems.shape[0]
    y_count, shares, half, tile = weights.shape
    spans = y_count // steps
    part = rows_buffer.shape[1] // steps
    height = sources[0].shape[0]
    copies = []
    for step in range(steps):
        features = pl.ds(step * part, part)
        chunk = [
            pltpu.make_async_copy(
                source.at[:, features],
                rows_buffer.at[pl.ds(i * height, height), features],
                row_sems.at[i, step],
            )
            for i, source in enumerate(sources)
        ]
        blocks = pl.ds(step * spans, spans)
        chunk.append(
            pltpu.make_async_copy(weight_source.at[blocks], weights.at[blocks], weight_sems.at[step])
        )
        copies.append(chunk)
    for chunk in copies:
        for copy in chunk:
            copy.start()
    for step in range(steps):
        for copy in copies[step]:
            copy.wait()
        tiles = [
            jnp.concatenate(
                [weights[span, lax.rem(2 * pair + c + shares - start, shares)] for c in range(2)],
                axis=0,
            )
            for span in range(step * spans, (step + 1) * spans)
            for pair in range(shares // 2)
        ]
        partial = lax.dot_general(
            rows_buffer[:, step * part : (step + 1) * part],
            jnp.concatenate(tiles, axis=1),
            (((1,), (1,)), ((), ())),
            preferred_element_type=jnp.float32,
        )
        if step == 0:
            total[...] = partial
        else:
            total[...] += partial


def turned(shards, total, rows_buffer):
    rows = total.shape[0]
    depth = rows // shards
    to = lax.broadcasted_iota(jnp.int32, (rows, rows), 0)
    source = lax.broadcasted_iota(jnp.int32, (rows, rows), 1)
    turn = (source == (to % depth) * shards + to // depth).astype(jnp.bfloat16)
    empty = rows_buffer[:, :128].astype(jnp.float32)[:, 0:1] > EMPTY_FROM
    kept = jnp.where(empty, EMPTY, total[...]).astype(jnp.bfloat16)
    return jnp.dot(turn, kept, preferred_element_type=jnp.float32).astype(jnp.bfloat16)


def first_kernel(shards, count, place_ref, *refs):
    out_ref, rows_buffer, weights, total, row_sems, weight_sems = refs[count + 1 :]
    block_product(place_ref[1], refs[:count], refs[count], rows_buffer, weights, total, row_sems, weight_sems)
    out_ref[...] = turned(shards, total, rows_buffer)


def second_kernel(shards, count, place_ref, first_ref, *refs):
    out_ref, rows_buffer, weights, total, row_sems, weight_sems = refs[count + 1 :]
    block_product(place_ref[1], refs[:count], refs[count], rows_buffer, weights, total, row_sems, weight_sems)
    width = total.shape[1]
    mine = first_ref[...]
    other = turned(shards, total, rows_buffer)

    @pl.when(place_ref[0] == 0)
    def _():
        out_ref[:, :width] = mine
        out_ref[:, width:] = other

    @pl.when(place_ref[0] != 0)
    def _():
        out_ref[:, :width] = other
        out_ref[:, width:] = mine


def product(place, pieces, weights, shards, first=None):
    y_count, shares, half, tile = weights.shape
    width = 2 * half
    depth = y_count * (shares // 2) * tile
    count = len(pieces)
    total_rows = pieces[0].shape[0] * count
    steps = 4
    joined = first is not None
    in_vmem = pl.BlockSpec(memory_space=pltpu.VMEM)
    head = [pl.BlockSpec(memory_space=pltpu.SMEM)] + ([in_vmem] if joined else [])
    kernel = second_kernel if joined else first_kernel
    return pl.pallas_call(
        functools.partial(kernel, shards, count),
        out_shape=jax.ShapeDtypeStruct(
            (total_rows, 2 * width if joined else width), jnp.bfloat16
        ),
        in_specs=head + [pl.BlockSpec(memory_space=pl.ANY)] * (count + 1),
        out_specs=in_vmem,
        scratch_shapes=[
            pltpu.VMEM((total_rows, depth), jnp.bfloat16),
            pltpu.VMEM(weights.shape, jnp.bfloat16),
            pltpu.VMEM((total_rows, width), jnp.float32),
            pltpu.SemaphoreType.DMA((count, steps)),
            pltpu.SemaphoreType.DMA((steps,)),
        ],
        compiler_params=pltpu.CompilerParams(vmem_limit_bytes=56 * MIB),
        cost_estimate=pl.CostEstimate(
            flops=2 * total_rows * depth * width,
            bytes_accessed=2 * depth * (total_rows + width),
            transcendentals=0,
        ),
    )(place, *((first,) if joined else ()), *pieces, weights)


def finish_kernel(
    mp_count, received_ref, hidden_ref, gain_ref, gradient_ref, message_ref, weighted_sum, gain_sum
):
    y_count, x_count, deep, quarter = received_ref.shape
    rows, width = hidden_ref.shape
    capacity = deep // x_count
    spans = [slice(x * quarter, (x + 1) * quarter) for x in range(x_count)]
    total = jnp.zeros((rows, 1), jnp.float32)
    for span in spans:
        values = hidden_ref[:, span].astype(jnp.float32)
        total += jnp.sum(values * values, axis=1, keepdims=True)
    inverse_rms = lax.rsqrt(total * (1.0 / width) + EPSILON)
    to = lax.broadcasted_iota(jnp.int32, (rows, rows), 0)
    source = lax.broadcasted_iota(jnp.int32, (rows, rows), 1)

    def rank_of(row, x):
        y, j, rank = row // deep, (row // capacity) % x_count, row % capacity
        return (y * x_count + (x - j + x_count) % x_count) * capacity + rank

    row_terms = jnp.zeros((rows, 1), jnp.float32)
    squares = jnp.zeros((rows, 1), jnp.float32)
    tally = None
    for x, span in enumerate(spans):
        block = received_ref[:, x].reshape(y_count * deep, quarter)
        live = jnp.where(block[:, 0:1].astype(jnp.float32) < EMPTY_FROM, 1.0, 0.0)
        live = jnp.broadcast_to(live, (rows, rows))
        if tally is None:
            tally = jnp.sum(live, axis=0, keepdims=True)[:, 0:1]
            filled = (
                lax.broadcasted_iota(jnp.int32, (rows, 1), 0).astype(jnp.float32) < tally
            ).astype(jnp.float32)
        before = (rank_of(source, x) < rank_of(to, x)).astype(jnp.bfloat16)
        slot = jnp.dot(before, live.astype(jnp.bfloat16), preferred_element_type=jnp.float32)
        chooser = jnp.where(slot == source.astype(jnp.float32), live, 0.0).astype(jnp.bfloat16)
        target = lax.dot_general(
            chooser, block, (((0,), (0,)), ((), ())), preferred_element_type=jnp.float32
        )
        gain = gain_ref[:, span]
        normal = hidden_ref[:, span].astype(jnp.float32) * inverse_rms
        mismatch = (normal * gain - target) * filled
        weighted = mismatch * gain
        weighted_sum[:, span] = weighted
        row_terms += jnp.sum(weighted * normal, axis=1, keepdims=True)
        squares += jnp.sum(mismatch * mismatch, axis=1, keepdims=True)
        gain_sum[:, span] = jnp.sum(mismatch * normal, axis=0, keepdims=True)
    row_mean = row_terms * (1.0 / width)
    for span in spans:
        normal = hidden_ref[:, span].astype(jnp.float32) * inverse_rms
        gradient_ref[:, span] = (
            inverse_rms * (weighted_sum[:, span] - normal * row_mean)
        ).astype(jnp.bfloat16)
    share = width // mp_count
    square_sum = jnp.sum(squares, axis=0, keepdims=True)
    lane = lax.broadcasted_iota(jnp.int32, (1, message_ref.shape[2] - share), 1)
    tail = jnp.where(lane == 0, square_sum, jnp.where(lane == 1, tally, 0.0))
    for m in range(mp_count):
        message_ref[m, :, :share] = gain_sum[:, m * share : (m + 1) * share]
        message_ref[m, :, share:] = tail


def finish(received, hidden, gains, mp_count):
    rows, width = hidden.shape
    share = width // mp_count
    in_vmem = pl.BlockSpec(memory_space=pltpu.VMEM)
    return pl.pallas_call(
        functools.partial(finish_kernel, mp_count),
        out_shape=(
            jax.ShapeDtypeStruct((rows, width), jnp.bfloat16),
            jax.ShapeDtypeStruct((mp_count, 1, share + 64), jnp.float32),
        ),
        in_specs=[in_vmem] * 3,
        out_specs=(in_vmem, in_vmem),
        scratch_shapes=[
            pltpu.VMEM((rows, width), jnp.float32),
            pltpu.VMEM((1, width), jnp.float32),
        ],
        compiler_params=pltpu.CompilerParams(vmem_limit_bytes=16 * MIB),
        cost_estimate=pl.CostEstimate(
            flops=2 * rows * rows * width, bytes_accessed=6 * rows * width, transcendentals=rows
        ),
    )(received, hidden, gains[None, :])


def ring_gather(top, low, x_count, dp_count):
    forward = [(d, d - d % x_count + (d + 1) % x_count) for d in range(dp_count)]
    backward = [(d, d - d % x_count + (d - 1) % x_count) for d in range(dp_count)]
    left_top = lax.ppermute(top, "dp", forward)
    right_low = lax.ppermute(low, "dp", backward)
    left_low = lax.ppermute(low, "dp", forward)
    right_top = lax.ppermute(top, "dp", backward)
    far_top = lax.ppermute(left_top, "dp", forward)
    far_low = lax.ppermute(right_low, "dp", backward)
    return [top, low, left_top, left_low, far_top, far_low, right_top, right_low]


def projector_columns(projector, student_gain, after, mp_count, x_count, y_count):
    core = lax.axis_index("group")
    dp_count = x_count * y_count
    columns = projector.T
    half, tile = columns.shape[0] // 2, columns.shape[1]
    share = lax.dynamic_slice_in_dim(columns, core * half, half, 0)
    moves = []
    for c in range(2):
        for d in range(dp_count):
            for z in range(mp_count):
                source = (c * dp_count + d) * mp_count + z
                y, x = divmod(d, x_count)
                to_d = y * x_count + z // 2
                moves.append((source, ((z % 2) * dp_count + to_d) * mp_count + 2 * x + c))
    piece = lax.ppermute(share, ("group", "dp", "mp"), moves)
    high = lax.reduce_precision(student_gain, 8, 7)
    middle = lax.reduce_precision(student_gain - high, 8, 7)
    low = student_gain - high - middle
    width = student_gain.shape[0]
    extra = 16
    parts = jnp.concatenate(
        [high, middle, low, jnp.zeros((extra * tile - 3 * width,), jnp.float32)]
    ).astype(jnp.bfloat16)
    held = jnp.concatenate([piece, parts.reshape(extra, tile)], axis=0)[None]
    while held.shape[0] < mp_count:
        step = held.shape[0]
        passed = lax.ppermute(held, "mp", [(z, (z - step) % mp_count) for z in range(mp_count)])
        held = jnp.concatenate([held, passed], axis=0)
    parts = held[:, half:].reshape(mp_count, extra * tile).astype(jnp.float32)
    gains = parts[:, :width] + parts[:, width : 2 * width] + parts[:, 2 * width : 3 * width]
    gains = lax.dynamic_slice_in_dim(
        jnp.concatenate([gains, gains], axis=0), mp_count - lax.axis_index("mp"), mp_count, 0
    )
    tiles = held[:, :half].reshape(mp_count * half, tile)
    tiles, _ = lax.optimization_barrier((tiles, after))
    y_groups = [[y * x_count + x for y in range(y_count)] for x in range(x_count)]
    mine = lax.all_gather(tiles, "dp", axis=0, axis_index_groups=y_groups, tiled=True)
    return mine.reshape(y_count, mp_count, half, tile), gains.reshape(mp_count * width)


def local(teacher_hidden, teacher_gain, projector, live, placement, student_hidden, student_gain):
    dp_count = lax.axis_size("dp")
    mp_count = lax.axis_size("mp")
    group_count = lax.axis_size("group")
    x_count = RING
    y_count = dp_count // x_count
    column = lax.axis_index("mp")
    core = lax.axis_index("group")
    slot_count = student_hidden.shape[0]
    capacity = slot_count // dp_count
    share_width = student_gain.shape[0]
    width = share_width * mp_count

    features = teacher_hidden.shape[1]
    blocks = teacher_hidden.reshape(mp_count, slot_count, features)
    moved = lax.all_to_all(blocks, "mp", 0, 0, tiled=True)
    mine, gains = projector_columns(projector, student_gain, moved, mp_count, x_count, y_count)

    own_live = lax.dynamic_index_in_dim(live.reshape(mp_count, slot_count), column, 0, keepdims=False)
    own_shards = lax.dynamic_index_in_dim(placement.reshape(mp_count, slot_count), column, 0, keepdims=False)
    order = jnp.arange(slot_count, dtype=jnp.int32)
    same = (
        (own_shards[:, None] == own_shards[None, :])
        & (own_live[:, None] == 1)
        & (order[:, None] < order[None, :])
    )
    rank = jnp.sum(same.astype(jnp.int32), axis=0)
    slot = jnp.where(own_live == 1, rank * dp_count + own_shards, -1)

    top, low = norm_rows(moved, slot, teacher_gain)
    pieces = ring_gather(top, low, x_count, dp_count)
    mine, pieces = lax.optimization_barrier((mine, pieces))
    other = lax.ppermute(mine, "group", [(0, 1), (1, 0)])
    place = jnp.stack([core, column]).astype(jnp.int32)
    first = product(place, pieces, mine, dp_count)
    buffer = product(place, pieces, other, dp_count, first)
    quarter = buffer.shape[1]
    deep = x_count * capacity
    received = lax.all_to_all(
        buffer.reshape(dp_count, deep, quarter), "dp", 0, 0, tiled=True
    ).reshape(y_count, x_count, deep, quarter)
    gradient, message = finish(received, student_hidden, gains, mp_count)

    over_mp = jnp.sum(lax.all_to_all(message, "mp", 0, 0, tiled=True), axis=(0, 1))
    peers = group_count * dp_count
    totals = jnp.sum(
        lax.all_to_all(
            jnp.broadcast_to(over_mp[None, :], (peers, over_mp.shape[0])), ("group", "dp"), 0, 0, tiled=True
        ),
        axis=0,
    )
    square_sum = totals[share_width]
    tally_sum = totals[share_width + 1]
    grad_gain = totals[:share_width] / tally_sum
    mean_loss = square_sum / (2.0 * tally_sum * width)
    return (gradient, grad_gain, mean_loss)


def solution(mesh):
    placed = (
        P(("group", "dp"), "mp"),
        P(),
        P("dp", "mp"),
        P(("group", "dp")),
        P(("group", "dp")),
        P(("group", "dp", "mp"), None),
        P("mp"),
    )
    return jax.shard_map(
        local,
        mesh=mesh,
        in_specs=placed,
        out_specs=(P(("group", "dp", "mp"), None), P("mp"), P()),
        check_vma=False,
    )
```

```python
import functools

import jax
import jax.numpy as jnp
from jax import lax
from jax.experimental import pallas as pl
from jax.experimental.pallas import tpu as pltpu
from jax.sharding import PartitionSpec as P

EPSILON = 1e-06
RING = 4
MIB = 1024 * 1024
FIRST_MIB = 44
SECOND_MIB = 16
EMPTY = 1e30
EMPTY_FROM = 1e20


def norm_kernel(moved_ref, slot_ref, gain_ref, top_ref, low_ref, packed):
    parts, rows, features = moved_ref.shape
    order = lax.broadcasted_iota(jnp.int32, (rows, rows), 0)
    packer = (order == slot_ref[...]).astype(jnp.bfloat16)
    total = jnp.zeros((rows, 1), jnp.float32)
    for part in range(parts):
        values = jnp.dot(packer, moved_ref[part], preferred_element_type=jnp.float32)
        packed[part] = values
        total += jnp.sum(values * values, axis=1, keepdims=True)
    inverse_rms = lax.rsqrt(total * (1.0 / (parts * features)) + EPSILON)
    half = rows // 2
    taken = jnp.sum(packer.astype(jnp.float32), axis=1, keepdims=True)
    first_column = lax.broadcasted_iota(jnp.int32, (rows, features), 1) == 0
    for part in range(parts):
        columns = slice(part * features, (part + 1) * features)
        normed = packed[part] * inverse_rms * gain_ref[:, columns]
        if part == 0:
            normed = jnp.where(first_column & (taken == 0.0), EMPTY, normed)
        normed = normed.astype(jnp.bfloat16)
        top_ref[:, columns] = normed[:half]
        low_ref[:, columns] = normed[half:]


def norm_rows(moved, slot, teacher_gain):
    parts, rows, features = moved.shape
    half = jax.ShapeDtypeStruct((rows // 2, parts * features), jnp.bfloat16)
    return pl.pallas_call(
        norm_kernel,
        out_shape=(half, half),
        scratch_shapes=[pltpu.VMEM((parts, rows, features), jnp.float32)],
        compiler_params=pltpu.CompilerParams(vmem_limit_bytes=16 * MIB),
        cost_estimate=pl.CostEstimate(
            flops=2 * rows * rows * parts * features,
            bytes_accessed=4 * rows * parts * features,
            transcendentals=rows,
        ),
    )(moved, slot[None, :], teacher_gain[None, :])


def block_dot(rows, weights, half, spans, pairs):
    tile = weights.shape[3]
    tiles = [
        weights[span, 2 * pair : 2 * pair + 2, :half].reshape(2 * half, tile)
        for span in spans
        for pair in range(pairs)
    ]
    return lax.dot_general(
        rows,
        jnp.concatenate(tiles, axis=1),
        (((1,), (1,)), ((), ())),
        preferred_element_type=jnp.float32,
    )


def block_product(rows, weights, half, total, steps, ready):
    y_count, shares = weights.shape[:2]
    spans = y_count // steps
    part = rows.shape[1] // steps
    for step in range(steps):
        ready(step)
        partial = block_dot(
            rows[:, step * part : (step + 1) * part],
            weights,
            half,
            range(step * spans, (step + 1) * spans),
            shares // 2,
        )
        if step == 0:
            total[...] = partial
        else:
            total[...] += partial


def turned(shards, total, all_rows):
    rows = total.shape[0]
    depth = rows // shards
    to = lax.broadcasted_iota(jnp.int32, (rows, rows), 0)
    source = lax.broadcasted_iota(jnp.int32, (rows, rows), 1)
    turn = (source == (to % depth) * shards + to // depth).astype(jnp.bfloat16)
    empty = all_rows[:, :128].astype(jnp.float32)[:, 0:1] > EMPTY_FROM
    kept = jnp.where(empty, EMPTY, total[...]).astype(jnp.bfloat16)
    return jnp.dot(turn, kept, preferred_element_type=jnp.float32).astype(jnp.bfloat16)


def first_kernel(shards, half, count, *refs):
    sources, weight_source = refs[:count], refs[count]
    out_ref, rows_ref, weights, total, row_sems, weight_sems = refs[count + 1 :]
    steps = weight_sems.shape[0]
    spans = weights.shape[0] // steps
    part = rows_ref.shape[1] // steps
    height = sources[0].shape[0]
    copies = []
    for step in range(steps):
        features = pl.ds(step * part, part)
        chunk = [
            pltpu.make_async_copy(
                source.at[:, features],
                rows_ref.at[pl.ds(i * height, height), features],
                row_sems.at[i, step],
            )
            for i, source in enumerate(sources)
        ]
        blocks = pl.ds(step * spans, spans)
        chunk.append(
            pltpu.make_async_copy(weight_source.at[blocks], weights.at[blocks], weight_sems.at[step])
        )
        copies.append(chunk)
    for chunk in copies:
        for copy in chunk:
            copy.start()

    def ready(step):
        for copy in copies[step]:
            copy.wait()

    block_product(rows_ref, weights, half, total, steps, ready)
    out_ref[...] = turned(shards, total, rows_ref)


def first_product(pieces, weights, half, shards):
    y_count, shares, _, tile = weights.shape
    depth = y_count * (shares // 2) * tile
    count = len(pieces)
    total_rows = pieces[0].shape[0] * count
    steps = 4
    in_vmem = pl.BlockSpec(memory_space=pltpu.VMEM)
    return pl.pallas_call(
        functools.partial(first_kernel, shards, half, count),
        out_shape=(
            jax.ShapeDtypeStruct((total_rows, 2 * half), jnp.bfloat16),
            jax.ShapeDtypeStruct((total_rows, depth), jnp.bfloat16),
        ),
        in_specs=[pl.BlockSpec(memory_space=pl.ANY)] * (count + 1),
        out_specs=(in_vmem, in_vmem),
        scratch_shapes=[
            pltpu.VMEM(weights.shape, jnp.bfloat16),
            pltpu.VMEM((total_rows, 2 * half), jnp.float32),
            pltpu.SemaphoreType.DMA((count, steps)),
            pltpu.SemaphoreType.DMA((steps,)),
        ],
        compiler_params=pltpu.CompilerParams(vmem_limit_bytes=FIRST_MIB * MIB),
        cost_estimate=pl.CostEstimate(
            flops=4 * total_rows * depth * half,
            bytes_accessed=2 * depth * (total_rows + 2 * half),
            transcendentals=0,
        ),
    )(*pieces, weights)


def second_kernel(shards, half, core_ref, first_ref, rows_ref, weights_ref, out_ref, total):
    block_product(rows_ref, weights_ref, half, total, 2, lambda step: None)
    width = total.shape[1]
    mine = first_ref[...]
    other = turned(shards, total, rows_ref)

    @pl.when(core_ref[0] == 0)
    def _():
        out_ref[:, :width] = mine
        out_ref[:, width:] = other

    @pl.when(core_ref[0] != 0)
    def _():
        out_ref[:, :width] = other
        out_ref[:, width:] = mine


def second_product(core, first, rows, weights, half, shards):
    total_rows, depth = rows.shape
    in_vmem = pl.BlockSpec(memory_space=pltpu.VMEM)
    return pl.pallas_call(
        functools.partial(second_kernel, shards, half),
        out_shape=jax.ShapeDtypeStruct((total_rows, 4 * half), jnp.bfloat16),
        in_specs=[pl.BlockSpec(memory_space=pltpu.SMEM)] + [in_vmem] * 3,
        out_specs=in_vmem,
        scratch_shapes=[pltpu.VMEM((total_rows, 2 * half), jnp.float32)],
        compiler_params=pltpu.CompilerParams(vmem_limit_bytes=SECOND_MIB * MIB),
        cost_estimate=pl.CostEstimate(
            flops=4 * total_rows * depth * half,
            bytes_accessed=2 * depth * (total_rows + 2 * half),
            transcendentals=0,
        ),
    )(core, first, rows, weights)


def finish_kernel(
    mp_count, received_ref, hidden_ref, gain_ref, gradient_ref, message_ref, weighted_sum, gain_sum
):
    y_count, x_count, deep, quarter = received_ref.shape
    rows, width = hidden_ref.shape
    capacity = deep // x_count
    spans = [slice(x * quarter, (x + 1) * quarter) for x in range(x_count)]
    total = jnp.zeros((rows, 1), jnp.float32)
    for span in spans:
        values = hidden_ref[:, span].astype(jnp.float32)
        total += jnp.sum(values * values, axis=1, keepdims=True)
    inverse_rms = lax.rsqrt(total * (1.0 / width) + EPSILON)
    to = lax.broadcasted_iota(jnp.int32, (rows, rows), 0)
    source = lax.broadcasted_iota(jnp.int32, (rows, rows), 1)

    def rank_of(row, x):
        y, j, rank = row // deep, (row // capacity) % x_count, row % capacity
        return (y * x_count + (x - j + x_count) % x_count) * capacity + rank

    row_terms = jnp.zeros((rows, 1), jnp.float32)
    squares = jnp.zeros((rows, 1), jnp.float32)
    tally = None
    for x, span in enumerate(spans):
        block = received_ref[:, x].reshape(y_count * deep, quarter)
        live = jnp.where(block[:, 0:1].astype(jnp.float32) < EMPTY_FROM, 1.0, 0.0)
        live = jnp.broadcast_to(live, (rows, rows))
        if tally is None:
            tally = jnp.sum(live, axis=0, keepdims=True)[:, 0:1]
            filled = (
                lax.broadcasted_iota(jnp.int32, (rows, 1), 0).astype(jnp.float32) < tally
            ).astype(jnp.float32)
        before = (rank_of(source, x) < rank_of(to, x)).astype(jnp.bfloat16)
        slot = jnp.dot(before, live.astype(jnp.bfloat16), preferred_element_type=jnp.float32)
        chooser = jnp.where(slot == source.astype(jnp.float32), live, 0.0).astype(jnp.bfloat16)
        target = lax.dot_general(
            chooser, block, (((0,), (0,)), ((), ())), preferred_element_type=jnp.float32
        )
        gain = gain_ref[:, span]
        normal = hidden_ref[:, span].astype(jnp.float32) * inverse_rms
        mismatch = (normal * gain - target) * filled
        weighted = mismatch * gain
        weighted_sum[:, span] = weighted
        row_terms += jnp.sum(weighted * normal, axis=1, keepdims=True)
        squares += jnp.sum(mismatch * mismatch, axis=1, keepdims=True)
        gain_sum[:, span] = jnp.sum(mismatch * normal, axis=0, keepdims=True)
    row_mean = row_terms * (1.0 / width)
    for span in spans:
        normal = hidden_ref[:, span].astype(jnp.float32) * inverse_rms
        gradient_ref[:, span] = (
            inverse_rms * (weighted_sum[:, span] - normal * row_mean)
        ).astype(jnp.bfloat16)
    share = width // mp_count
    square_sum = jnp.sum(squares, axis=0, keepdims=True)
    lane = lax.broadcasted_iota(jnp.int32, (1, message_ref.shape[2] - share), 1)
    tail = jnp.where(lane == 0, square_sum, jnp.where(lane == 1, tally, 0.0))
    for m in range(mp_count):
        message_ref[m, :, :share] = gain_sum[:, m * share : (m + 1) * share]
        message_ref[m, :, share:] = tail


def finish(received, hidden, gains, mp_count):
    rows, width = hidden.shape
    share = width // mp_count
    in_vmem = pl.BlockSpec(memory_space=pltpu.VMEM)
    return pl.pallas_call(
        functools.partial(finish_kernel, mp_count),
        out_shape=(
            jax.ShapeDtypeStruct((rows, width), jnp.bfloat16),
            jax.ShapeDtypeStruct((mp_count, 1, share + 64), jnp.float32),
        ),
        in_specs=[in_vmem] * 3,
        out_specs=(in_vmem, in_vmem),
        scratch_shapes=[
            pltpu.VMEM((rows, width), jnp.float32),
            pltpu.VMEM((1, width), jnp.float32),
        ],
        compiler_params=pltpu.CompilerParams(vmem_limit_bytes=16 * MIB),
        cost_estimate=pl.CostEstimate(
            flops=2 * rows * rows * width, bytes_accessed=6 * rows * width, transcendentals=rows
        ),
    )(received, hidden, gains[None, :])


def ring_gather(top, low, x_count, dp_count):
    forward = [(d, d - d % x_count + (d + 1) % x_count) for d in range(dp_count)]
    backward = [(d, d - d % x_count + (d - 1) % x_count) for d in range(dp_count)]
    left_top = lax.ppermute(top, "dp", forward)
    right_low = lax.ppermute(low, "dp", backward)
    left_low = lax.ppermute(low, "dp", forward)
    right_top = lax.ppermute(top, "dp", backward)
    far_top = lax.ppermute(left_top, "dp", forward)
    far_low = lax.ppermute(right_low, "dp", backward)
    return [top, low, left_top, left_low, far_top, far_low, right_top, right_low]


def projector_columns(projector, student_gain, mp_count, x_count, y_count):
    core = lax.axis_index("group")
    dp_count = x_count * y_count
    columns = projector.T
    half, tile = columns.shape[0] // 2, columns.shape[1]
    share = lax.dynamic_slice_in_dim(columns, core * half, half, 0)
    moves = []
    for c in range(2):
        for d in range(dp_count):
            for z in range(mp_count):
                source = (c * dp_count + d) * mp_count + z
                y, x = divmod(d, x_count)
                to_d = y * x_count + z // 2
                moves.append((source, ((z % 2) * dp_count + to_d) * mp_count + 2 * x + c))
    piece = lax.ppermute(share, ("group", "dp", "mp"), moves)
    high = lax.reduce_precision(student_gain, 8, 7)
    middle = lax.reduce_precision(student_gain - high, 8, 7)
    low = student_gain - high - middle
    width = student_gain.shape[0]
    extra = 16
    parts = jnp.concatenate(
        [high, middle, low, jnp.zeros((extra * tile - 3 * width,), jnp.float32)]
    ).astype(jnp.bfloat16)
    message = jnp.concatenate([piece, parts.reshape(extra, tile)], axis=0)
    spread = lax.all_to_all(
        jnp.broadcast_to(message[None], (mp_count,) + message.shape), "mp", 0, 0, tiled=True
    )
    parts = spread[:, half:].reshape(mp_count, extra * tile).astype(jnp.float32)
    gains = parts[:, :width] + parts[:, width : 2 * width] + parts[:, 2 * width : 3 * width]
    tiles = spread.reshape(mp_count * (half + extra), tile)
    y_groups = [[y * x_count + x for y in range(y_count)] for x in range(x_count)]
    mine = lax.all_gather(tiles, "dp", axis=0, axis_index_groups=y_groups, tiled=True)
    return mine.reshape(y_count, mp_count, half + extra, tile), gains.reshape(mp_count * width)


def local(teacher_hidden, teacher_gain, projector, live, placement, student_hidden, student_gain):
    dp_count = lax.axis_size("dp")
    mp_count = lax.axis_size("mp")
    group_count = lax.axis_size("group")
    x_count = RING
    y_count = dp_count // x_count
    column = lax.axis_index("mp")
    core = lax.axis_index("group")
    slot_count = student_hidden.shape[0]
    capacity = slot_count // dp_count
    share_width = student_gain.shape[0]
    width = share_width * mp_count

    features = teacher_hidden.shape[1]
    blocks = teacher_hidden.reshape(mp_count, slot_count, features)
    moved = lax.all_to_all(blocks, "mp", 0, 0, tiled=True)
    mine, gains = projector_columns(projector, student_gain, mp_count, x_count, y_count)

    own_live = lax.dynamic_index_in_dim(live.reshape(mp_count, slot_count), column, 0, keepdims=False)
    own_shards = lax.dynamic_index_in_dim(placement.reshape(mp_count, slot_count), column, 0, keepdims=False)
    order = jnp.arange(slot_count, dtype=jnp.int32)
    same = (
        (own_shards[:, None] == own_shards[None, :])
        & (own_live[:, None] == 1)
        & (order[:, None] < order[None, :])
    )
    rank = jnp.sum(same.astype(jnp.int32), axis=0)
    slot = jnp.where(own_live == 1, rank * dp_count + own_shards, -1)

    top, low = norm_rows(moved, slot, teacher_gain)
    pieces = ring_gather(top, low, x_count, dp_count)
    mine, pieces = lax.optimization_barrier((mine, pieces))
    other = lax.ppermute(mine, "group", [(0, 1), (1, 0)])
    half = share_width // 2
    first, rows = first_product(pieces, mine, half, dp_count)
    place = core.astype(jnp.int32).reshape(1)
    buffer = second_product(place, first, rows, other, half, dp_count)
    quarter = buffer.shape[1]
    deep = x_count * capacity
    received = lax.all_to_all(
        buffer.reshape(dp_count, deep, quarter), "dp", 0, 0, tiled=True
    ).reshape(y_count, x_count, deep, quarter)
    gradient, message = finish(received, student_hidden, gains, mp_count)

    over_mp = jnp.sum(lax.all_to_all(message, "mp", 0, 0, tiled=True), axis=(0, 1))
    peers = group_count * dp_count
    totals = jnp.sum(
        lax.all_to_all(
            jnp.broadcast_to(over_mp[None, :], (peers, over_mp.shape[0])), ("group", "dp"), 0, 0, tiled=True
        ),
        axis=0,
    )
    square_sum = totals[share_width]
    tally_sum = totals[share_width + 1]
    grad_gain = totals[:share_width] / tally_sum
    mean_loss = square_sum / (2.0 * tally_sum * width)
    return (gradient, grad_gain, mean_loss)


def solution(mesh):
    placed = (
        P(("group", "dp"), "mp"),
        P(),
        P("dp", "mp"),
        P(("group", "dp")),
        P(("group", "dp")),
        P(("group", "dp", "mp"), None),
        P("mp"),
    )
    return jax.shard_map(
        local,
        mesh=mesh,
        in_specs=placed,
        out_specs=(P(("group", "dp", "mp"), None), P("mp"), P()),
        check_vma=False,
    )
```

```python
import functools

import jax
import jax.numpy as jnp
from jax import lax
from jax.experimental import pallas as pl
from jax.experimental.pallas import tpu as pltpu
from jax.sharding import PartitionSpec as P

EPSILON = 1e-06
RING = 4
MIB = 1024 * 1024
EMPTY = 1e30
EMPTY_FROM = 1e20


def norm_kernel(moved_ref, slot_ref, gain_ref, top_ref, low_ref, packed):
    parts, rows, features = moved_ref.shape
    order = lax.broadcasted_iota(jnp.int32, (rows, rows), 0)
    packer = (order == slot_ref[...]).astype(jnp.bfloat16)
    total = jnp.zeros((rows, 1), jnp.float32)
    for part in range(parts):
        values = jnp.dot(packer, moved_ref[part], preferred_element_type=jnp.float32)
        packed[part] = values
        total += jnp.sum(values * values, axis=1, keepdims=True)
    inverse_rms = lax.rsqrt(total * (1.0 / (parts * features)) + EPSILON)
    half = rows // 2
    taken = jnp.sum(packer.astype(jnp.float32), axis=1, keepdims=True)
    first_column = lax.broadcasted_iota(jnp.int32, (rows, features), 1) == 0
    for part in range(parts):
        columns = slice(part * features, (part + 1) * features)
        normed = packed[part] * inverse_rms * gain_ref[:, columns]
        if part == 0:
            normed = jnp.where(first_column & (taken == 0.0), EMPTY, normed)
        normed = normed.astype(jnp.bfloat16)
        top_ref[:, columns] = normed[:half]
        low_ref[:, columns] = normed[half:]


def norm_rows(moved, slot, teacher_gain):
    parts, rows, features = moved.shape
    half = jax.ShapeDtypeStruct((rows // 2, parts * features), jnp.bfloat16)
    return pl.pallas_call(
        norm_kernel,
        out_shape=(half, half),
        scratch_shapes=[pltpu.VMEM((parts, rows, features), jnp.float32)],
        compiler_params=pltpu.CompilerParams(vmem_limit_bytes=16 * MIB),
        cost_estimate=pl.CostEstimate(
            flops=2 * rows * rows * parts * features,
            bytes_accessed=4 * rows * parts * features,
            transcendentals=rows,
        ),
    )(moved, slot[None, :], teacher_gain[None, :])


def block_dot(rows, weights, half, spans, pairs):
    tile = weights.shape[3]
    tiles = [
        weights[span, 2 * pair : 2 * pair + 2, :half].reshape(2 * half, tile)
        for span in spans
        for pair in range(pairs)
    ]
    return lax.dot_general(
        rows,
        jnp.concatenate(tiles, axis=1),
        (((1,), (1,)), ((), ())),
        preferred_element_type=jnp.float32,
    )


def block_product(pieces, weights, half, total):
    y_count, shares = weights.shape[:2]
    steps = 4
    spans = y_count // steps
    part = pieces[0].shape[1] // steps
    for step in range(steps):
        features = slice(step * part, (step + 1) * part)
        partial = block_dot(
            jnp.concatenate([piece[:, features] for piece in pieces], axis=0),
            weights,
            half,
            range(step * spans, (step + 1) * spans),
            shares // 2,
        )
        if step == 0:
            total[...] = partial
        else:
            total[...] += partial


def turned(shards, total, pieces):
    rows = total.shape[0]
    depth = rows // shards
    to = lax.broadcasted_iota(jnp.int32, (rows, rows), 0)
    source = lax.broadcasted_iota(jnp.int32, (rows, rows), 1)
    turn = (source == (to % depth) * shards + to // depth).astype(jnp.bfloat16)
    first_features = jnp.concatenate([piece[:, :128] for piece in pieces], axis=0)
    empty = first_features.astype(jnp.float32)[:, 0:1] > EMPTY_FROM
    kept = jnp.where(empty, EMPTY, total[...]).astype(jnp.bfloat16)
    return jnp.dot(turn, kept, preferred_element_type=jnp.float32).astype(jnp.bfloat16)


def first_kernel(shards, half, count, *refs):
    pieces, weights_ref, out_ref, total = refs[:count], *refs[count:]
    block_product(pieces, weights_ref, half, total)
    out_ref[...] = turned(shards, total, pieces)


def second_kernel(shards, half, count, core_ref, first_ref, *refs):
    pieces, weights_ref, out_ref, total = refs[:count], *refs[count:]
    block_product(pieces, weights_ref, half, total)
    width = total.shape[1]
    mine = first_ref[...]
    other = turned(shards, total, pieces)

    @pl.when(core_ref[0] == 0)
    def _():
        out_ref[:, :width] = mine
        out_ref[:, width:] = other

    @pl.when(core_ref[0] != 0)
    def _():
        out_ref[:, :width] = other
        out_ref[:, width:] = mine


def product(pieces, weights, half, shards, core=None, first=None):
    y_count, shares, _, tile = weights.shape
    depth = y_count * (shares // 2) * tile
    count = len(pieces)
    total_rows = pieces[0].shape[0] * count
    joined = first is not None
    in_vmem = pl.BlockSpec(memory_space=pltpu.VMEM)
    head = [pl.BlockSpec(memory_space=pltpu.SMEM), in_vmem] if joined else []
    kernel = second_kernel if joined else first_kernel
    return pl.pallas_call(
        functools.partial(kernel, shards, half, count),
        out_shape=jax.ShapeDtypeStruct(
            (total_rows, (4 if joined else 2) * half), jnp.bfloat16
        ),
        in_specs=head + [in_vmem] * (count + 1),
        out_specs=in_vmem,
        scratch_shapes=[pltpu.VMEM((total_rows, 2 * half), jnp.float32)],
        compiler_params=pltpu.CompilerParams(vmem_limit_bytes=32 * MIB),
        cost_estimate=pl.CostEstimate(
            flops=4 * total_rows * depth * half,
            bytes_accessed=2 * depth * (total_rows + 2 * half),
            transcendentals=0,
        ),
    )(*((core, first) if joined else ()), *pieces, weights)


def finish_kernel(
    mp_count, received_ref, hidden_ref, gain_ref, gradient_ref, message_ref, weighted_sum, gain_sum
):
    y_count, x_count, deep, quarter = received_ref.shape
    rows, width = hidden_ref.shape
    capacity = deep // x_count
    spans = [slice(x * quarter, (x + 1) * quarter) for x in range(x_count)]
    total = jnp.zeros((rows, 1), jnp.float32)
    for span in spans:
        values = hidden_ref[:, span].astype(jnp.float32)
        total += jnp.sum(values * values, axis=1, keepdims=True)
    inverse_rms = lax.rsqrt(total * (1.0 / width) + EPSILON)
    to = lax.broadcasted_iota(jnp.int32, (rows, rows), 0)
    source = lax.broadcasted_iota(jnp.int32, (rows, rows), 1)

    def rank_of(row, x):
        y, j, rank = row // deep, (row // capacity) % x_count, row % capacity
        return (y * x_count + (x - j + x_count) % x_count) * capacity + rank

    row_terms = jnp.zeros((rows, 1), jnp.float32)
    squares = jnp.zeros((rows, 1), jnp.float32)
    tally = None
    for x, span in enumerate(spans):
        block = received_ref[:, x].reshape(y_count * deep, quarter)
        live = jnp.where(block[:, 0:1].astype(jnp.float32) < EMPTY_FROM, 1.0, 0.0)
        live = jnp.broadcast_to(live, (rows, rows))
        if tally is None:
            tally = jnp.sum(live, axis=0, keepdims=True)[:, 0:1]
            filled = (
                lax.broadcasted_iota(jnp.int32, (rows, 1), 0).astype(jnp.float32) < tally
            ).astype(jnp.float32)
        before = (rank_of(source, x) < rank_of(to, x)).astype(jnp.bfloat16)
        slot = jnp.dot(before, live.astype(jnp.bfloat16), preferred_element_type=jnp.float32)
        chooser = jnp.where(slot == source.astype(jnp.float32), live, 0.0).astype(jnp.bfloat16)
        target = lax.dot_general(
            chooser, block, (((0,), (0,)), ((), ())), preferred_element_type=jnp.float32
        )
        gain = gain_ref[:, span]
        normal = hidden_ref[:, span].astype(jnp.float32) * inverse_rms
        mismatch = (normal * gain - target) * filled
        weighted = mismatch * gain
        weighted_sum[:, span] = weighted
        row_terms += jnp.sum(weighted * normal, axis=1, keepdims=True)
        squares += jnp.sum(mismatch * mismatch, axis=1, keepdims=True)
        gain_sum[:, span] = jnp.sum(mismatch * normal, axis=0, keepdims=True)
    row_mean = row_terms * (1.0 / width)
    for span in spans:
        normal = hidden_ref[:, span].astype(jnp.float32) * inverse_rms
        gradient_ref[:, span] = (
            inverse_rms * (weighted_sum[:, span] - normal * row_mean)
        ).astype(jnp.bfloat16)
    share = width // mp_count
    square_sum = jnp.sum(squares, axis=0, keepdims=True)
    lane = lax.broadcasted_iota(jnp.int32, (1, message_ref.shape[2] - share), 1)
    tail = jnp.where(lane == 0, square_sum, jnp.where(lane == 1, tally, 0.0))
    for m in range(mp_count):
        message_ref[m, :, :share] = gain_sum[:, m * share : (m + 1) * share]
        message_ref[m, :, share:] = tail


def finish(received, hidden, gains, mp_count):
    rows, width = hidden.shape
    share = width // mp_count
    in_vmem = pl.BlockSpec(memory_space=pltpu.VMEM)
    return pl.pallas_call(
        functools.partial(finish_kernel, mp_count),
        out_shape=(
            jax.ShapeDtypeStruct((rows, width), jnp.bfloat16),
            jax.ShapeDtypeStruct((mp_count, 1, share + 64), jnp.float32),
        ),
        in_specs=[in_vmem] * 3,
        out_specs=(in_vmem, in_vmem),
        scratch_shapes=[
            pltpu.VMEM((rows, width), jnp.float32),
            pltpu.VMEM((1, width), jnp.float32),
        ],
        compiler_params=pltpu.CompilerParams(vmem_limit_bytes=16 * MIB),
        cost_estimate=pl.CostEstimate(
            flops=2 * rows * rows * width, bytes_accessed=6 * rows * width, transcendentals=rows
        ),
    )(received, hidden, gains[None, :])


def ring_gather(top, low, x_count, dp_count):
    forward = [(d, d - d % x_count + (d + 1) % x_count) for d in range(dp_count)]
    backward = [(d, d - d % x_count + (d - 1) % x_count) for d in range(dp_count)]
    left_top = lax.ppermute(top, "dp", forward)
    right_low = lax.ppermute(low, "dp", backward)
    left_low = lax.ppermute(low, "dp", forward)
    right_top = lax.ppermute(top, "dp", backward)
    far_top = lax.ppermute(left_top, "dp", forward)
    far_low = lax.ppermute(right_low, "dp", backward)
    return [top, low, left_top, left_low, far_top, far_low, right_top, right_low]


def projector_columns(projector, student_gain, mp_count, x_count, y_count):
    core = lax.axis_index("group")
    dp_count = x_count * y_count
    columns = projector.T
    half, tile = columns.shape[0] // 2, columns.shape[1]
    share = lax.dynamic_slice_in_dim(columns, core * half, half, 0)
    moves = []
    for c in range(2):
        for d in range(dp_count):
            for z in range(mp_count):
                source = (c * dp_count + d) * mp_count + z
                y, x = divmod(d, x_count)
                to_d = y * x_count + z // 2
                moves.append((source, ((z % 2) * dp_count + to_d) * mp_count + 2 * x + c))
    piece = lax.ppermute(share, ("group", "dp", "mp"), moves)
    high = lax.reduce_precision(student_gain, 8, 7)
    middle = lax.reduce_precision(student_gain - high, 8, 7)
    low = student_gain - high - middle
    width = student_gain.shape[0]
    extra = 16
    parts = jnp.concatenate(
        [high, middle, low, jnp.zeros((extra * tile - 3 * width,), jnp.float32)]
    ).astype(jnp.bfloat16)
    message = jnp.concatenate([piece, parts.reshape(extra, tile)], axis=0)
    spread = lax.all_to_all(
        jnp.broadcast_to(message[None], (mp_count,) + message.shape), "mp", 0, 0, tiled=True
    )
    parts = spread[:, half:].reshape(mp_count, extra * tile).astype(jnp.float32)
    gains = parts[:, :width] + parts[:, width : 2 * width] + parts[:, 2 * width : 3 * width]
    tiles = spread.reshape(mp_count * (half + extra), tile)
    y_groups = [[y * x_count + x for y in range(y_count)] for x in range(x_count)]
    mine = lax.all_gather(tiles, "dp", axis=0, axis_index_groups=y_groups, tiled=True)
    return mine.reshape(y_count, mp_count, half + extra, tile), gains.reshape(mp_count * width)


def local(teacher_hidden, teacher_gain, projector, live, placement, student_hidden, student_gain):
    dp_count = lax.axis_size("dp")
    mp_count = lax.axis_size("mp")
    group_count = lax.axis_size("group")
    x_count = RING
    y_count = dp_count // x_count
    column = lax.axis_index("mp")
    core = lax.axis_index("group")
    slot_count = student_hidden.shape[0]
    capacity = slot_count // dp_count
    share_width = student_gain.shape[0]
    width = share_width * mp_count

    features = teacher_hidden.shape[1]
    blocks = teacher_hidden.reshape(mp_count, slot_count, features)
    moved = lax.all_to_all(blocks, "mp", 0, 0, tiled=True)
    mine, gains = projector_columns(projector, student_gain, mp_count, x_count, y_count)

    own_live = lax.dynamic_index_in_dim(live.reshape(mp_count, slot_count), column, 0, keepdims=False)
    own_shards = lax.dynamic_index_in_dim(placement.reshape(mp_count, slot_count), column, 0, keepdims=False)
    order = jnp.arange(slot_count, dtype=jnp.int32)
    same = (
        (own_shards[:, None] == own_shards[None, :])
        & (own_live[:, None] == 1)
        & (order[:, None] < order[None, :])
    )
    rank = jnp.sum(same.astype(jnp.int32), axis=0)
    slot = jnp.where(own_live == 1, rank * dp_count + own_shards, -1)

    top, low = norm_rows(moved, slot, teacher_gain)
    pieces = ring_gather(top, low, x_count, dp_count)
    mine, pieces = lax.optimization_barrier((mine, pieces))
    other = lax.ppermute(mine, "group", [(0, 1), (1, 0)])
    half = share_width // 2
    first = product(pieces, mine, half, dp_count)
    place = core.astype(jnp.int32).reshape(1)
    buffer = product(pieces, other, half, dp_count, place, first)
    quarter = buffer.shape[1]
    deep = x_count * capacity
    received = lax.all_to_all(
        buffer.reshape(dp_count, deep, quarter), "dp", 0, 0, tiled=True
    ).reshape(y_count, x_count, deep, quarter)
    gradient, message = finish(received, student_hidden, gains, mp_count)

    over_mp = jnp.sum(lax.all_to_all(message, "mp", 0, 0, tiled=True), axis=(0, 1))
    peers = group_count * dp_count
    totals = jnp.sum(
        lax.all_to_all(
            jnp.broadcast_to(over_mp[None, :], (peers, over_mp.shape[0])), ("group", "dp"), 0, 0, tiled=True
        ),
        axis=0,
    )
    square_sum = totals[share_width]
    tally_sum = totals[share_width + 1]
    grad_gain = totals[:share_width] / tally_sum
    mean_loss = square_sum / (2.0 * tally_sum * width)
    return (gradient, grad_gain, mean_loss)


def solution(mesh):
    placed = (
        P(("group", "dp"), "mp"),
        P(),
        P("dp", "mp"),
        P(("group", "dp")),
        P(("group", "dp")),
        P(("group", "dp", "mp"), None),
        P("mp"),
    )
    return jax.shard_map(
        local,
        mesh=mesh,
        in_specs=placed,
        out_specs=(P(("group", "dp", "mp"), None), P("mp"), P()),
        check_vma=False,
    )
```

```python
import functools

import jax
import jax.numpy as jnp
from jax import lax
from jax.experimental import pallas as pl
from jax.experimental.pallas import tpu as pltpu
from jax.sharding import PartitionSpec as P

EPSILON = 1e-06
RING = 4
MIB = 1024 * 1024
EMPTY = 1e30
EMPTY_FROM = 1e20


def norm_kernel(moved_ref, slot_ref, gain_ref, top_ref, low_ref, packed):
    parts, rows, features = moved_ref.shape
    order = lax.broadcasted_iota(jnp.int32, (rows, rows), 0)
    packer = (order == slot_ref[...]).astype(jnp.bfloat16)
    total = jnp.zeros((rows, 1), jnp.float32)
    for part in range(parts):
        values = jnp.dot(packer, moved_ref[part], preferred_element_type=jnp.float32)
        packed[part] = values
        total += jnp.sum(values * values, axis=1, keepdims=True)
    inverse_rms = lax.rsqrt(total * (1.0 / (parts * features)) + EPSILON)
    half = rows // 2
    taken = jnp.sum(packer.astype(jnp.float32), axis=1, keepdims=True)
    first_column = lax.broadcasted_iota(jnp.int32, (rows, features), 1) == 0
    for part in range(parts):
        columns = slice(part * features, (part + 1) * features)
        normed = packed[part] * inverse_rms * gain_ref[:, columns]
        if part == 0:
            normed = jnp.where(first_column & (taken == 0.0), EMPTY, normed)
        normed = normed.astype(jnp.bfloat16)
        top_ref[:, columns] = normed[:half]
        low_ref[:, columns] = normed[half:]


def norm_rows(moved, slot, teacher_gain):
    parts, rows, features = moved.shape
    half = jax.ShapeDtypeStruct((rows // 2, parts * features), jnp.bfloat16)
    return pl.pallas_call(
        norm_kernel,
        out_shape=(half, half),
        scratch_shapes=[pltpu.VMEM((parts, rows, features), jnp.float32)],
        compiler_params=pltpu.CompilerParams(vmem_limit_bytes=16 * MIB),
        cost_estimate=pl.CostEstimate(
            flops=2 * rows * rows * parts * features,
            bytes_accessed=4 * rows * parts * features,
            transcendentals=rows,
        ),
    )(moved, slot[None, :], teacher_gain[None, :])


def block_dot(rows, weights, half, spans, pairs):
    tile = weights.shape[3]
    tiles = [
        weights[span, 2 * pair : 2 * pair + 2, :half].reshape(2 * half, tile)
        for span in spans
        for pair in range(pairs)
    ]
    return lax.dot_general(
        rows,
        jnp.concatenate(tiles, axis=1),
        (((1,), (1,)), ((), ())),
        preferred_element_type=jnp.float32,
    )


def block_product(pieces, weights, half, total):
    y_count, shares = weights.shape[:2]
    steps = 4
    spans = y_count // steps
    part = pieces[0].shape[1] // steps
    for step in range(steps):
        features = slice(step * part, (step + 1) * part)
        partial = block_dot(
            jnp.concatenate([piece[:, features] for piece in pieces], axis=0),
            weights,
            half,
            range(step * spans, (step + 1) * spans),
            shares // 2,
        )
        if step == 0:
            total[...] = partial
        else:
            total[...] += partial


def turned(shards, total, pieces):
    rows = total.shape[0]
    depth = rows // shards
    to = lax.broadcasted_iota(jnp.int32, (rows, rows), 0)
    source = lax.broadcasted_iota(jnp.int32, (rows, rows), 1)
    turn = (source == (to % depth) * shards + to // depth).astype(jnp.bfloat16)
    first_features = jnp.concatenate([piece[:, :128] for piece in pieces], axis=0)
    empty = first_features.astype(jnp.float32)[:, 0:1] > EMPTY_FROM
    kept = jnp.where(empty, EMPTY, total[...]).astype(jnp.bfloat16)
    return jnp.dot(turn, kept, preferred_element_type=jnp.float32).astype(jnp.bfloat16)


def first_kernel(shards, half, count, *refs):
    pieces, weights_ref, out_ref, total = refs[:count], *refs[count:]
    block_product(pieces, weights_ref, half, total)
    out_ref[...] = turned(shards, total, pieces)


def second_kernel(shards, half, count, core_ref, first_ref, *refs):
    pieces, weights_ref, out_ref, total = refs[:count], *refs[count:]
    block_product(pieces, weights_ref, half, total)
    width = total.shape[1]
    mine = first_ref[...]
    other = turned(shards, total, pieces)

    @pl.when(core_ref[0] == 0)
    def _():
        out_ref[:, :width] = mine
        out_ref[:, width:] = other

    @pl.when(core_ref[0] != 0)
    def _():
        out_ref[:, :width] = other
        out_ref[:, width:] = mine


def product(pieces, weights, half, shards, core=None, first=None):
    y_count, shares, _, tile = weights.shape
    depth = y_count * (shares // 2) * tile
    count = len(pieces)
    total_rows = pieces[0].shape[0] * count
    joined = first is not None
    in_vmem = pl.BlockSpec(memory_space=pltpu.VMEM)
    head = [pl.BlockSpec(memory_space=pltpu.SMEM), in_vmem] if joined else []
    kernel = second_kernel if joined else first_kernel
    return pl.pallas_call(
        functools.partial(kernel, shards, half, count),
        out_shape=jax.ShapeDtypeStruct(
            (total_rows, (4 if joined else 2) * half), jnp.bfloat16
        ),
        in_specs=head + [in_vmem] * (count + 1),
        out_specs=in_vmem,
        scratch_shapes=[pltpu.VMEM((total_rows, 2 * half), jnp.float32)],
        compiler_params=pltpu.CompilerParams(vmem_limit_bytes=32 * MIB),
        cost_estimate=pl.CostEstimate(
            flops=4 * total_rows * depth * half,
            bytes_accessed=2 * depth * (total_rows + 2 * half),
            transcendentals=0,
        ),
    )(*((core, first) if joined else ()), *pieces, weights)


def finish_kernel(
    mp_count, received_ref, hidden_ref, gain_ref, gradient_ref, message_ref, weighted_sum, gain_sum
):
    y_count, x_count, deep, quarter = received_ref.shape
    rows, width = hidden_ref.shape
    capacity = deep // x_count
    spans = [slice(x * quarter, (x + 1) * quarter) for x in range(x_count)]
    total = jnp.zeros((rows, 1), jnp.float32)
    for span in spans:
        values = hidden_ref[:, span].astype(jnp.float32)
        total += jnp.sum(values * values, axis=1, keepdims=True)
    inverse_rms = lax.rsqrt(total * (1.0 / width) + EPSILON)
    to = lax.broadcasted_iota(jnp.int32, (rows, rows), 0)
    source = lax.broadcasted_iota(jnp.int32, (rows, rows), 1)

    def rank_of(row, x):
        y, j, rank = row // deep, (row // capacity) % x_count, row % capacity
        return (y * x_count + (x - j + x_count) % x_count) * capacity + rank

    row_terms = jnp.zeros((rows, 1), jnp.float32)
    squares = jnp.zeros((rows, 1), jnp.float32)
    tally = None
    for x, span in enumerate(spans):
        block = received_ref[:, x].reshape(y_count * deep, quarter)
        live = jnp.where(block[:, 0:1].astype(jnp.float32) < EMPTY_FROM, 1.0, 0.0)
        live = jnp.broadcast_to(live, (rows, rows))
        if tally is None:
            tally = jnp.sum(live, axis=0, keepdims=True)[:, 0:1]
            filled = (
                lax.broadcasted_iota(jnp.int32, (rows, 1), 0).astype(jnp.float32) < tally
            ).astype(jnp.float32)
        before = (rank_of(source, x) < rank_of(to, x)).astype(jnp.bfloat16)
        slot = jnp.dot(before, live.astype(jnp.bfloat16), preferred_element_type=jnp.float32)
        chooser = jnp.where(slot == source.astype(jnp.float32), live, 0.0).astype(jnp.bfloat16)
        target = lax.dot_general(
            chooser, block, (((0,), (0,)), ((), ())), preferred_element_type=jnp.float32
        )
        gain = gain_ref[:, span]
        normal = hidden_ref[:, span].astype(jnp.float32) * inverse_rms
        mismatch = (normal * gain - target) * filled
        weighted = mismatch * gain
        weighted_sum[:, span] = weighted
        row_terms += jnp.sum(weighted * normal, axis=1, keepdims=True)
        squares += jnp.sum(mismatch * mismatch, axis=1, keepdims=True)
        gain_sum[:, span] = jnp.sum(mismatch * normal, axis=0, keepdims=True)
    row_mean = row_terms * (1.0 / width)
    for span in spans:
        normal = hidden_ref[:, span].astype(jnp.float32) * inverse_rms
        gradient_ref[:, span] = (
            inverse_rms * (weighted_sum[:, span] - normal * row_mean)
        ).astype(jnp.bfloat16)
    share = width // mp_count
    square_sum = jnp.sum(squares, axis=0, keepdims=True)
    lane = lax.broadcasted_iota(jnp.int32, (1, message_ref.shape[2] - share), 1)
    tail = jnp.where(lane == 0, square_sum, jnp.where(lane == 1, tally, 0.0))
    for m in range(mp_count):
        message_ref[m, :, :share] = gain_sum[:, m * share : (m + 1) * share]
        message_ref[m, :, share:] = tail


def finish(received, hidden, gains, mp_count):
    rows, width = hidden.shape
    share = width // mp_count
    in_vmem = pl.BlockSpec(memory_space=pltpu.VMEM)
    return pl.pallas_call(
        functools.partial(finish_kernel, mp_count),
        out_shape=(
            jax.ShapeDtypeStruct((rows, width), jnp.bfloat16),
            jax.ShapeDtypeStruct((mp_count, 1, share + 64), jnp.float32),
        ),
        in_specs=[in_vmem] * 3,
        out_specs=(in_vmem, in_vmem),
        scratch_shapes=[
            pltpu.VMEM((rows, width), jnp.float32),
            pltpu.VMEM((1, width), jnp.float32),
        ],
        compiler_params=pltpu.CompilerParams(vmem_limit_bytes=16 * MIB),
        cost_estimate=pl.CostEstimate(
            flops=2 * rows * rows * width, bytes_accessed=6 * rows * width, transcendentals=rows
        ),
    )(received, hidden, gains[None, :])


def last_kernel(share, width, parts_ref, gain_ref, loss_ref):
    total = jnp.sum(parts_ref[...], axis=0)
    tally = total[:, share + 1 : share + 2]
    gain_ref[...] = total[:, :share] / tally
    loss_ref[...] = total[:, share : share + 1] / (2.0 * tally * width)


def last(parts, share, width):
    in_vmem = pl.BlockSpec(memory_space=pltpu.VMEM)
    return pl.pallas_call(
        functools.partial(last_kernel, share, float(width)),
        out_shape=(
            jax.ShapeDtypeStruct((1, share), jnp.float32),
            jax.ShapeDtypeStruct((1, 1), jnp.float32),
        ),
        in_specs=[in_vmem],
        out_specs=(in_vmem, in_vmem),
        compiler_params=pltpu.CompilerParams(vmem_limit_bytes=4 * MIB),
    )(parts)


def ring_gather(top, low, x_count, dp_count):
    forward = [(d, d - d % x_count + (d + 1) % x_count) for d in range(dp_count)]
    backward = [(d, d - d % x_count + (d - 1) % x_count) for d in range(dp_count)]
    left_top = lax.ppermute(top, "dp", forward)
    right_low = lax.ppermute(low, "dp", backward)
    left_low = lax.ppermute(low, "dp", forward)
    right_top = lax.ppermute(top, "dp", backward)
    far_top = lax.ppermute(left_top, "dp", forward)
    far_low = lax.ppermute(right_low, "dp", backward)
    return [top, low, left_top, left_low, far_top, far_low, right_top, right_low]


def projector_columns(projector, student_gain, mp_count, x_count, y_count):
    core = lax.axis_index("group")
    dp_count = x_count * y_count
    columns = projector.T
    half, tile = columns.shape[0] // 2, columns.shape[1]
    share = lax.dynamic_slice_in_dim(columns, core * half, half, 0)
    moves = []
    for c in range(2):
        for d in range(dp_count):
            for z in range(mp_count):
                source = (c * dp_count + d) * mp_count + z
                y, x = divmod(d, x_count)
                to_d = y * x_count + z // 2
                moves.append((source, ((z % 2) * dp_count + to_d) * mp_count + 2 * x + c))
    piece = lax.ppermute(share, ("group", "dp", "mp"), moves)
    high = lax.reduce_precision(student_gain, 8, 7)
    middle = lax.reduce_precision(student_gain - high, 8, 7)
    low = student_gain - high - middle
    width = student_gain.shape[0]
    extra = 16
    parts = jnp.concatenate(
        [high, middle, low, jnp.zeros((extra * tile - 3 * width,), jnp.float32)]
    ).astype(jnp.bfloat16)
    message = jnp.concatenate([piece, parts.reshape(extra, tile)], axis=0)
    spread = lax.all_to_all(
        jnp.broadcast_to(message[None], (mp_count,) + message.shape), "mp", 0, 0, tiled=True
    )
    parts = spread[:, half:].reshape(mp_count, extra * tile).astype(jnp.float32)
    gains = parts[:, :width] + parts[:, width : 2 * width] + parts[:, 2 * width : 3 * width]
    tiles = spread.reshape(mp_count * (half + extra), tile)
    y_groups = [[y * x_count + x for y in range(y_count)] for x in range(x_count)]
    mine = lax.all_gather(tiles, "dp", axis=0, axis_index_groups=y_groups, tiled=True)
    return mine.reshape(y_count, mp_count, half + extra, tile), gains.reshape(mp_count * width)


def local(teacher_hidden, teacher_gain, projector, live, placement, student_hidden, student_gain):
    dp_count = lax.axis_size("dp")
    mp_count = lax.axis_size("mp")
    group_count = lax.axis_size("group")
    x_count = RING
    y_count = dp_count // x_count
    column = lax.axis_index("mp")
    core = lax.axis_index("group")
    slot_count = student_hidden.shape[0]
    capacity = slot_count // dp_count
    share_width = student_gain.shape[0]
    width = share_width * mp_count

    features = teacher_hidden.shape[1]
    blocks = teacher_hidden.reshape(mp_count, slot_count, features)
    moved = lax.all_to_all(blocks, "mp", 0, 0, tiled=True)
    mine, gains = projector_columns(projector, student_gain, mp_count, x_count, y_count)

    own_live = lax.dynamic_index_in_dim(live.reshape(mp_count, slot_count), column, 0, keepdims=False)
    own_shards = lax.dynamic_index_in_dim(placement.reshape(mp_count, slot_count), column, 0, keepdims=False)
    order = jnp.arange(slot_count, dtype=jnp.int32)
    same = (
        (own_shards[:, None] == own_shards[None, :])
        & (own_live[:, None] == 1)
        & (order[:, None] < order[None, :])
    )
    rank = jnp.sum(same.astype(jnp.int32), axis=0)
    slot = jnp.where(own_live == 1, rank * dp_count + own_shards, -1)

    top, low = norm_rows(moved, slot, teacher_gain)
    pieces = ring_gather(top, low, x_count, dp_count)
    mine, pieces = lax.optimization_barrier((mine, pieces))
    other = lax.ppermute(mine, "group", [(0, 1), (1, 0)])
    half = share_width // 2
    first = product(pieces, mine, half, dp_count)
    place = core.astype(jnp.int32).reshape(1)
    buffer = product(pieces, other, half, dp_count, place, first)
    quarter = buffer.shape[1]
    deep = x_count * capacity
    received = lax.all_to_all(
        buffer.reshape(dp_count, deep, quarter), "dp", 0, 0, tiled=True
    ).reshape(y_count, x_count, deep, quarter)
    gradient, message = finish(received, student_hidden, gains, mp_count)

    over_mp = jnp.sum(lax.all_to_all(message, "mp", 0, 0, tiled=True), axis=(0, 1))
    peers = group_count * dp_count
    parts = lax.all_to_all(
        jnp.broadcast_to(over_mp[None, None, :], (peers, 1, over_mp.shape[0])),
        ("group", "dp"),
        0,
        0,
        tiled=True,
    )
    grad_gain, mean_loss = last(parts, share_width, width)
    return (gradient, grad_gain.reshape(share_width), mean_loss.reshape(()))


def solution(mesh):
    placed = (
        P(("group", "dp"), "mp"),
        P(),
        P("dp", "mp"),
        P(("group", "dp")),
        P(("group", "dp")),
        P(("group", "dp", "mp"), None),
        P("mp"),
    )
    return jax.shard_map(
        local,
        mesh=mesh,
        in_specs=placed,
        out_specs=(P(("group", "dp", "mp"), None), P("mp"), P()),
        check_vma=False,
    )
```

```python
import functools

import jax
import jax.numpy as jnp
from jax import lax
from jax.experimental import pallas as pl
from jax.experimental.pallas import tpu as pltpu
from jax.sharding import PartitionSpec as P

EPSILON = 1e-06
RING = 4
MIB = 1024 * 1024
EMPTY = 1e30
EMPTY_FROM = 1e20


def norm_kernel(moved_ref, slot_ref, gain_ref, top_ref, low_ref, packed):
    parts, rows, features = moved_ref.shape
    order = lax.broadcasted_iota(jnp.int32, (rows, rows), 0)
    packer = (order == slot_ref[...]).astype(jnp.bfloat16)
    total = jnp.zeros((rows, 1), jnp.float32)
    for part in range(parts):
        values = jnp.dot(packer, moved_ref[part], preferred_element_type=jnp.float32)
        packed[part] = values
        total += jnp.sum(values * values, axis=1, keepdims=True)
    inverse_rms = lax.rsqrt(total * (1.0 / (parts * features)) + EPSILON)
    half = rows // 2
    taken = jnp.sum(packer.astype(jnp.float32), axis=1, keepdims=True)
    first_column = lax.broadcasted_iota(jnp.int32, (rows, features), 1) == 0
    for part in range(parts):
        columns = slice(part * features, (part + 1) * features)
        normed = packed[part] * inverse_rms * gain_ref[:, columns]
        if part == 0:
            normed = jnp.where(first_column & (taken == 0.0), EMPTY, normed)
        normed = normed.astype(jnp.bfloat16)
        top_ref[:, columns] = normed[:half]
        low_ref[:, columns] = normed[half:]


def norm_rows(moved, slot, teacher_gain):
    parts, rows, features = moved.shape
    half = jax.ShapeDtypeStruct((rows // 2, parts * features), jnp.bfloat16)
    return pl.pallas_call(
        norm_kernel,
        out_shape=(half, half),
        scratch_shapes=[pltpu.VMEM((parts, rows, features), jnp.float32)],
        compiler_params=pltpu.CompilerParams(vmem_limit_bytes=16 * MIB),
        cost_estimate=pl.CostEstimate(
            flops=2 * rows * rows * parts * features,
            bytes_accessed=4 * rows * parts * features,
            transcendentals=rows,
        ),
    )(moved, slot[None, :], teacher_gain[None, :])


def block_dot(rows, weights, half, spans, pairs):
    tile = weights.shape[3]
    tiles = [
        weights[span, 2 * pair : 2 * pair + 2, :half].reshape(2 * half, tile)
        for span in spans
        for pair in range(pairs)
    ]
    return lax.dot_general(
        rows,
        jnp.concatenate(tiles, axis=1),
        (((1,), (1,)), ((), ())),
        preferred_element_type=jnp.float32,
    )


def block_product(pieces, weights, half, total):
    y_count, shares = weights.shape[:2]
    steps = 4
    spans = y_count // steps
    part = pieces[0].shape[1] // steps
    for step in range(steps):
        features = slice(step * part, (step + 1) * part)
        partial = block_dot(
            jnp.concatenate([piece[:, features] for piece in pieces], axis=0),
            weights,
            half,
            range(step * spans, (step + 1) * spans),
            shares // 2,
        )
        if step == 0:
            total[...] = partial
        else:
            total[...] += partial


def turned(shards, total, pieces):
    rows = total.shape[0]
    depth = rows // shards
    to = lax.broadcasted_iota(jnp.int32, (rows, rows), 0)
    source = lax.broadcasted_iota(jnp.int32, (rows, rows), 1)
    turn = (source == (to % depth) * shards + to // depth).astype(jnp.bfloat16)
    first_features = jnp.concatenate([piece[:, :128] for piece in pieces], axis=0)
    empty = first_features.astype(jnp.float32)[:, 0:1] > EMPTY_FROM
    kept = jnp.where(empty, EMPTY, total[...]).astype(jnp.bfloat16)
    return jnp.dot(turn, kept, preferred_element_type=jnp.float32).astype(jnp.bfloat16)


def first_kernel(shards, half, count, *refs):
    pieces, weights_ref, out_ref, total = refs[:count], *refs[count:]
    block_product(pieces, weights_ref, half, total)
    out_ref[...] = turned(shards, total, pieces)


def second_kernel(shards, half, count, core_ref, first_ref, *refs):
    pieces, weights_ref, out_ref, total = refs[:count], *refs[count:]
    block_product(pieces, weights_ref, half, total)
    width = total.shape[1]
    mine = first_ref[...]
    other = turned(shards, total, pieces)

    @pl.when(core_ref[0] == 0)
    def _():
        out_ref[:, :width] = mine
        out_ref[:, width:] = other

    @pl.when(core_ref[0] != 0)
    def _():
        out_ref[:, :width] = other
        out_ref[:, width:] = mine


def product(pieces, weights, half, shards, core=None, first=None):
    y_count, shares, _, tile = weights.shape
    depth = y_count * (shares // 2) * tile
    count = len(pieces)
    total_rows = pieces[0].shape[0] * count
    joined = first is not None
    in_vmem = pl.BlockSpec(memory_space=pltpu.VMEM)
    head = [pl.BlockSpec(memory_space=pltpu.SMEM), in_vmem] if joined else []
    kernel = second_kernel if joined else first_kernel
    return pl.pallas_call(
        functools.partial(kernel, shards, half, count),
        out_shape=jax.ShapeDtypeStruct(
            (total_rows, (4 if joined else 2) * half), jnp.bfloat16
        ),
        in_specs=head + [in_vmem] * (count + 1),
        out_specs=in_vmem,
        scratch_shapes=[pltpu.VMEM((total_rows, 2 * half), jnp.float32)],
        compiler_params=pltpu.CompilerParams(vmem_limit_bytes=32 * MIB),
        cost_estimate=pl.CostEstimate(
            flops=4 * total_rows * depth * half,
            bytes_accessed=2 * depth * (total_rows + 2 * half),
            transcendentals=0,
        ),
    )(*((core, first) if joined else ()), *pieces, weights)


def student_kernel(hidden_ref, normal_ref, rms_ref):
    rows, width = hidden_ref.shape
    quarter = width // 4
    spans = [slice(x * quarter, (x + 1) * quarter) for x in range(4)]
    total = jnp.zeros((rows, 1), jnp.float32)
    for span in spans:
        values = hidden_ref[:, span].astype(jnp.float32)
        total += jnp.sum(values * values, axis=1, keepdims=True)
    inverse_rms = lax.rsqrt(total * (1.0 / width) + EPSILON)
    for span in spans:
        normal_ref[:, span] = hidden_ref[:, span].astype(jnp.float32) * inverse_rms
    rms_ref[...] = jnp.broadcast_to(inverse_rms, rms_ref.shape)


def student_rows(hidden):
    rows, width = hidden.shape
    in_vmem = pl.BlockSpec(memory_space=pltpu.VMEM)
    return pl.pallas_call(
        student_kernel,
        out_shape=(
            jax.ShapeDtypeStruct((rows, width), jnp.float32),
            jax.ShapeDtypeStruct((rows, 128), jnp.float32),
        ),
        in_specs=[in_vmem],
        out_specs=(in_vmem, in_vmem),
        compiler_params=pltpu.CompilerParams(vmem_limit_bytes=16 * MIB),
        cost_estimate=pl.CostEstimate(
            flops=4 * rows * width, bytes_accessed=6 * rows * width, transcendentals=rows
        ),
    )(hidden)


def finish_kernel(
    mp_count, received_ref, normal_ref, rms_ref, gain_ref, gradient_ref, message_ref, weighted_sum, gain_sum
):
    y_count, x_count, deep, quarter = received_ref.shape
    rows, width = normal_ref.shape
    capacity = deep // x_count
    spans = [slice(x * quarter, (x + 1) * quarter) for x in range(x_count)]
    inverse_rms = rms_ref[:, 0:1]
    to = lax.broadcasted_iota(jnp.int32, (rows, rows), 0)
    source = lax.broadcasted_iota(jnp.int32, (rows, rows), 1)

    def rank_of(row, x):
        y, j, rank = row // deep, (row // capacity) % x_count, row % capacity
        return (y * x_count + (x - j + x_count) % x_count) * capacity + rank

    row_terms = jnp.zeros((rows, 1), jnp.float32)
    squares = jnp.zeros((rows, 1), jnp.float32)
    tally = None
    for x, span in enumerate(spans):
        block = received_ref[:, x].reshape(y_count * deep, quarter)
        live = jnp.where(block[:, 0:1].astype(jnp.float32) < EMPTY_FROM, 1.0, 0.0)
        live = jnp.broadcast_to(live, (rows, rows))
        if tally is None:
            tally = jnp.sum(live, axis=0, keepdims=True)[:, 0:1]
            filled = (
                lax.broadcasted_iota(jnp.int32, (rows, 1), 0).astype(jnp.float32) < tally
            ).astype(jnp.float32)
        before = (rank_of(source, x) < rank_of(to, x)).astype(jnp.bfloat16)
        slot = jnp.dot(before, live.astype(jnp.bfloat16), preferred_element_type=jnp.float32)
        chooser = jnp.where(slot == source.astype(jnp.float32), live, 0.0).astype(jnp.bfloat16)
        target = lax.dot_general(
            chooser, block, (((0,), (0,)), ((), ())), preferred_element_type=jnp.float32
        )
        gain = gain_ref[:, span]
        normal = normal_ref[:, span]
        mismatch = (normal * gain - target) * filled
        weighted = mismatch * gain
        weighted_sum[:, span] = weighted
        row_terms += jnp.sum(weighted * normal, axis=1, keepdims=True)
        squares += jnp.sum(mismatch * mismatch, axis=1, keepdims=True)
        gain_sum[:, span] = jnp.sum(mismatch * normal, axis=0, keepdims=True)
    row_mean = row_terms * (1.0 / width)
    for span in spans:
        normal = normal_ref[:, span]
        gradient_ref[:, span] = (
            inverse_rms * (weighted_sum[:, span] - normal * row_mean)
        ).astype(jnp.bfloat16)
    share = width // mp_count
    square_sum = jnp.sum(squares, axis=0, keepdims=True)
    lane = lax.broadcasted_iota(jnp.int32, (1, message_ref.shape[2] - share), 1)
    tail = jnp.where(lane == 0, square_sum, jnp.where(lane == 1, tally, 0.0))
    for m in range(mp_count):
        message_ref[m, :, :share] = gain_sum[:, m * share : (m + 1) * share]
        message_ref[m, :, share:] = tail


def finish(received, normal, inverse_rms, gains, mp_count):
    rows, width = normal.shape
    share = width // mp_count
    in_vmem = pl.BlockSpec(memory_space=pltpu.VMEM)
    return pl.pallas_call(
        functools.partial(finish_kernel, mp_count),
        out_shape=(
            jax.ShapeDtypeStruct((rows, width), jnp.bfloat16),
            jax.ShapeDtypeStruct((mp_count, 1, share + 64), jnp.float32),
        ),
        in_specs=[in_vmem] * 4,
        out_specs=(in_vmem, in_vmem),
        scratch_shapes=[
            pltpu.VMEM((rows, width), jnp.float32),
            pltpu.VMEM((1, width), jnp.float32),
        ],
        compiler_params=pltpu.CompilerParams(vmem_limit_bytes=16 * MIB),
        cost_estimate=pl.CostEstimate(
            flops=2 * rows * rows * width, bytes_accessed=6 * rows * width, transcendentals=rows
        ),
    )(received, normal, inverse_rms, gains[None, :])


def last_kernel(share, width, parts_ref, gain_ref, loss_ref):
    total = jnp.sum(parts_ref[...], axis=0)
    tally = total[:, share + 1 : share + 2]
    gain_ref[...] = total[:, :share] / tally
    loss_ref[...] = total[:, share : share + 1] / (2.0 * tally * width)


def last(parts, share, width):
    in_vmem = pl.BlockSpec(memory_space=pltpu.VMEM)
    return pl.pallas_call(
        functools.partial(last_kernel, share, float(width)),
        out_shape=(
            jax.ShapeDtypeStruct((1, share), jnp.float32),
            jax.ShapeDtypeStruct((1, 1), jnp.float32),
        ),
        in_specs=[in_vmem],
        out_specs=(in_vmem, in_vmem),
        compiler_params=pltpu.CompilerParams(vmem_limit_bytes=4 * MIB),
    )(parts)


def ring_gather(top, low, x_count, dp_count):
    forward = [(d, d - d % x_count + (d + 1) % x_count) for d in range(dp_count)]
    backward = [(d, d - d % x_count + (d - 1) % x_count) for d in range(dp_count)]
    left_top = lax.ppermute(top, "dp", forward)
    right_low = lax.ppermute(low, "dp", backward)
    left_low = lax.ppermute(low, "dp", forward)
    right_top = lax.ppermute(top, "dp", backward)
    far_top = lax.ppermute(left_top, "dp", forward)
    far_low = lax.ppermute(right_low, "dp", backward)
    return [top, low, left_top, left_low, far_top, far_low, right_top, right_low]


def projector_columns(projector, student_gain, mp_count, x_count, y_count):
    core = lax.axis_index("group")
    dp_count = x_count * y_count
    columns = projector.T
    half, tile = columns.shape[0] // 2, columns.shape[1]
    share = lax.dynamic_slice_in_dim(columns, core * half, half, 0)
    moves = []
    for c in range(2):
        for d in range(dp_count):
            for z in range(mp_count):
                source = (c * dp_count + d) * mp_count + z
                y, x = divmod(d, x_count)
                to_d = y * x_count + z // 2
                moves.append((source, ((z % 2) * dp_count + to_d) * mp_count + 2 * x + c))
    piece = lax.ppermute(share, ("group", "dp", "mp"), moves)
    high = lax.reduce_precision(student_gain, 8, 7)
    middle = lax.reduce_precision(student_gain - high, 8, 7)
    low = student_gain - high - middle
    width = student_gain.shape[0]
    extra = 16
    parts = jnp.concatenate(
        [high, middle, low, jnp.zeros((extra * tile - 3 * width,), jnp.float32)]
    ).astype(jnp.bfloat16)
    message = jnp.concatenate([piece, parts.reshape(extra, tile)], axis=0)
    spread = lax.all_to_all(
        jnp.broadcast_to(message[None], (mp_count,) + message.shape), "mp", 0, 0, tiled=True
    )
    parts = spread[:, half:].reshape(mp_count, extra * tile).astype(jnp.float32)
    gains = parts[:, :width] + parts[:, width : 2 * width] + parts[:, 2 * width : 3 * width]
    tiles = spread.reshape(mp_count * (half + extra), tile)
    y_groups = [[y * x_count + x for y in range(y_count)] for x in range(x_count)]
    mine = lax.all_gather(tiles, "dp", axis=0, axis_index_groups=y_groups, tiled=True)
    return mine.reshape(y_count, mp_count, half + extra, tile), gains.reshape(mp_count * width)


def local(teacher_hidden, teacher_gain, projector, live, placement, student_hidden, student_gain):
    dp_count = lax.axis_size("dp")
    mp_count = lax.axis_size("mp")
    group_count = lax.axis_size("group")
    x_count = RING
    y_count = dp_count // x_count
    column = lax.axis_index("mp")
    core = lax.axis_index("group")
    slot_count = student_hidden.shape[0]
    capacity = slot_count // dp_count
    share_width = student_gain.shape[0]
    width = share_width * mp_count

    features = teacher_hidden.shape[1]
    blocks = teacher_hidden.reshape(mp_count, slot_count, features)
    moved = lax.all_to_all(blocks, "mp", 0, 0, tiled=True)
    mine, gains = projector_columns(projector, student_gain, mp_count, x_count, y_count)

    own_live = lax.dynamic_index_in_dim(live.reshape(mp_count, slot_count), column, 0, keepdims=False)
    own_shards = lax.dynamic_index_in_dim(placement.reshape(mp_count, slot_count), column, 0, keepdims=False)
    order = jnp.arange(slot_count, dtype=jnp.int32)
    same = (
        (own_shards[:, None] == own_shards[None, :])
        & (own_live[:, None] == 1)
        & (order[:, None] < order[None, :])
    )
    rank = jnp.sum(same.astype(jnp.int32), axis=0)
    slot = jnp.where(own_live == 1, rank * dp_count + own_shards, -1)

    top, low = norm_rows(moved, slot, teacher_gain)
    pieces = ring_gather(top, low, x_count, dp_count)
    mine, pieces = lax.optimization_barrier((mine, pieces))
    other = lax.ppermute(mine, "group", [(0, 1), (1, 0)])
    half = share_width // 2
    first = product(pieces, mine, half, dp_count)
    place = core.astype(jnp.int32).reshape(1)
    buffer = product(pieces, other, half, dp_count, place, first)
    quarter = buffer.shape[1]
    deep = x_count * capacity
    received = lax.all_to_all(
        buffer.reshape(dp_count, deep, quarter), "dp", 0, 0, tiled=True
    ).reshape(y_count, x_count, deep, quarter)
    hidden, _ = lax.optimization_barrier((student_hidden, buffer))
    normal, inverse_rms = student_rows(hidden)
    gradient, message = finish(received, normal, inverse_rms, gains, mp_count)

    over_mp = jnp.sum(lax.all_to_all(message, "mp", 0, 0, tiled=True), axis=(0, 1))
    peers = group_count * dp_count
    parts = lax.all_to_all(
        jnp.broadcast_to(over_mp[None, None, :], (peers, 1, over_mp.shape[0])),
        ("group", "dp"),
        0,
        0,
        tiled=True,
    )
    grad_gain, mean_loss = last(parts, share_width, width)
    return (gradient, grad_gain.reshape(share_width), mean_loss.reshape(()))


def solution(mesh):
    placed = (
        P(("group", "dp"), "mp"),
        P(),
        P("dp", "mp"),
        P(("group", "dp")),
        P(("group", "dp")),
        P(("group", "dp", "mp"), None),
        P("mp"),
    )
    return jax.shard_map(
        local,
        mesh=mesh,
        in_specs=placed,
        out_specs=(P(("group", "dp", "mp"), None), P("mp"), P()),
        check_vma=False,
    )
```

```python
import functools

import jax
import jax.numpy as jnp
from jax import lax
from jax.experimental import pallas as pl
from jax.experimental.pallas import tpu as pltpu
from jax.sharding import PartitionSpec as P

EPSILON = 1e-06
RING = 4
MIB = 1024 * 1024
EMPTY = 1e30
EMPTY_FROM = 1e20


def norm_kernel(moved_ref, slot_ref, gain_ref, top_ref, low_ref, own_ref, packed):
    parts, rows, features = moved_ref.shape
    order = lax.broadcasted_iota(jnp.int32, (rows, rows), 0)
    packer = (order == slot_ref[...]).astype(jnp.bfloat16)
    total = jnp.zeros((rows, 1), jnp.float32)
    for part in range(parts):
        values = jnp.dot(packer, moved_ref[part], preferred_element_type=jnp.float32)
        packed[part] = values
        total += jnp.sum(values * values, axis=1, keepdims=True)
    inverse_rms = lax.rsqrt(total * (1.0 / (parts * features)) + EPSILON)
    half = rows // 2
    taken = jnp.sum(packer.astype(jnp.float32), axis=1, keepdims=True)
    first_column = lax.broadcasted_iota(jnp.int32, (rows, features), 1) == 0
    for part in range(parts):
        columns = slice(part * features, (part + 1) * features)
        normed = packed[part] * inverse_rms * gain_ref[:, columns]
        if part == 0:
            normed = jnp.where(first_column & (taken == 0.0), EMPTY, normed)
        normed = normed.astype(jnp.bfloat16)
        top_ref[:, columns] = normed[:half]
        low_ref[:, columns] = normed[half:]
        own_ref[:, columns] = normed


def norm_rows(moved, slot, teacher_gain):
    parts, rows, features = moved.shape
    half = jax.ShapeDtypeStruct((rows // 2, parts * features), jnp.bfloat16)
    return pl.pallas_call(
        norm_kernel,
        out_shape=(half, half, jax.ShapeDtypeStruct((rows, parts * features), jnp.bfloat16)),
        scratch_shapes=[pltpu.VMEM((parts, rows, features), jnp.float32)],
        compiler_params=pltpu.CompilerParams(vmem_limit_bytes=16 * MIB),
        cost_estimate=pl.CostEstimate(
            flops=2 * rows * rows * parts * features,
            bytes_accessed=4 * rows * parts * features,
            transcendentals=rows,
        ),
    )(moved, slot[None, :], teacher_gain[None, :])


def block_dot(rows, weights, half, spans, pairs):
    tile = weights.shape[3]
    tiles = [
        weights[span, 2 * pair : 2 * pair + 2, :half].reshape(2 * half, tile)
        for span in spans
        for pair in range(pairs)
    ]
    return lax.dot_general(
        rows,
        jnp.concatenate(tiles, axis=1),
        (((1,), (1,)), ((), ())),
        preferred_element_type=jnp.float32,
    )


def block_product(pieces, weights, half, total):
    y_count, shares = weights.shape[:2]
    steps = 4
    spans = y_count // steps
    part = pieces[0].shape[1] // steps
    for step in range(steps):
        features = slice(step * part, (step + 1) * part)
        partial = block_dot(
            jnp.concatenate([piece[:, features] for piece in pieces], axis=0),
            weights,
            half,
            range(step * spans, (step + 1) * spans),
            shares // 2,
        )
        if step == 0:
            total[...] = partial
        else:
            total[...] += partial


def turned(shards, total, pieces):
    rows = total.shape[0]
    depth = rows // shards
    to = lax.broadcasted_iota(jnp.int32, (rows, 1), 0)
    source = lax.broadcasted_iota(jnp.int32, (rows, rows), 1)
    turn = (source == (to % depth) * shards + to // depth).astype(jnp.bfloat16)
    first_features = jnp.concatenate([piece[:, :128] for piece in pieces], axis=0)
    empty = first_features.astype(jnp.float32)[:, 0:1] > EMPTY_FROM
    kept = jnp.where(empty, EMPTY, total[...]).astype(jnp.bfloat16)
    return jnp.dot(turn, kept, preferred_element_type=jnp.float32).astype(jnp.bfloat16)


def first_kernel(shards, half, count, *refs):
    pieces, weights_ref, out_ref, total = refs[:count], *refs[count:]
    block_product(pieces, weights_ref, half, total)
    out_ref[...] = turned(shards, total, pieces)


def second_kernel(shards, half, count, core_ref, first_ref, *refs):
    pieces, weights_ref, out_ref, total = refs[:count], *refs[count:]
    block_product(pieces, weights_ref, half, total)
    width = total.shape[1]
    mine = first_ref[...]
    other = turned(shards, total, pieces)

    @pl.when(core_ref[0] == 0)
    def _():
        out_ref[:, :width] = mine
        out_ref[:, width:] = other

    @pl.when(core_ref[0] != 0)
    def _():
        out_ref[:, :width] = other
        out_ref[:, width:] = mine


def product(pieces, weights, half, shards, core=None, first=None):
    y_count, shares, _, tile = weights.shape
    depth = y_count * (shares // 2) * tile
    count = len(pieces)
    total_rows = sum(piece.shape[0] for piece in pieces)
    joined = first is not None
    in_vmem = pl.BlockSpec(memory_space=pltpu.VMEM)
    head = [pl.BlockSpec(memory_space=pltpu.SMEM), in_vmem] if joined else []
    kernel = second_kernel if joined else first_kernel
    return pl.pallas_call(
        functools.partial(kernel, shards, half, count),
        out_shape=jax.ShapeDtypeStruct(
            (total_rows, (4 if joined else 2) * half), jnp.bfloat16
        ),
        in_specs=head + [in_vmem] * (count + 1),
        out_specs=in_vmem,
        scratch_shapes=[pltpu.VMEM((total_rows, 2 * half), jnp.float32)],
        compiler_params=pltpu.CompilerParams(vmem_limit_bytes=32 * MIB),
        cost_estimate=pl.CostEstimate(
            flops=4 * total_rows * depth * half,
            bytes_accessed=2 * depth * (total_rows + 2 * half),
            transcendentals=0,
        ),
    )(*((core, first) if joined else ()), *pieces, weights)


def student_kernel(hidden_ref, normal_ref, rms_ref):
    rows, width = hidden_ref.shape
    quarter = width // 4
    spans = [slice(x * quarter, (x + 1) * quarter) for x in range(4)]
    total = jnp.zeros((rows, 1), jnp.float32)
    for span in spans:
        values = hidden_ref[:, span].astype(jnp.float32)
        total += jnp.sum(values * values, axis=1, keepdims=True)
    inverse_rms = lax.rsqrt(total * (1.0 / width) + EPSILON)
    for span in spans:
        normal_ref[:, span] = hidden_ref[:, span].astype(jnp.float32) * inverse_rms
    rms_ref[...] = jnp.broadcast_to(inverse_rms, rms_ref.shape)


def student_rows(hidden):
    rows, width = hidden.shape
    in_vmem = pl.BlockSpec(memory_space=pltpu.VMEM)
    return pl.pallas_call(
        student_kernel,
        out_shape=(
            jax.ShapeDtypeStruct((rows, width), jnp.float32),
            jax.ShapeDtypeStruct((rows, 128), jnp.float32),
        ),
        in_specs=[in_vmem],
        out_specs=(in_vmem, in_vmem),
        compiler_params=pltpu.CompilerParams(vmem_limit_bytes=16 * MIB),
        cost_estimate=pl.CostEstimate(
            flops=4 * rows * width, bytes_accessed=6 * rows * width, transcendentals=rows
        ),
    )(hidden)


def finish_kernel(
    mp_count, received_ref, normal_ref, rms_ref, gain_ref, gradient_ref, message_ref, weighted_sum, gain_sum
):
    y_count, x_count, deep, quarter = received_ref.shape
    rows, width = normal_ref.shape
    capacity = deep // x_count
    spans = [slice(x * quarter, (x + 1) * quarter) for x in range(x_count)]
    inverse_rms = rms_ref[:, 0:1]
    to = lax.broadcasted_iota(jnp.int32, (rows, rows), 0)
    source = lax.broadcasted_iota(jnp.int32, (rows, rows), 1)

    def rank_of(row, x):
        y, j, rank = row // deep, (row // capacity) % x_count, row % capacity
        return (y * x_count + (x - j + x_count) % x_count) * capacity + rank

    row_terms = jnp.zeros((rows, 1), jnp.float32)
    squares = jnp.zeros((rows, 1), jnp.float32)
    tally = None
    for x, span in enumerate(spans):
        block = received_ref[:, x].reshape(y_count * deep, quarter)
        live = jnp.where(block[:, 0:1].astype(jnp.float32) < EMPTY_FROM, 1.0, 0.0)
        live = jnp.broadcast_to(live, (rows, rows))
        if tally is None:
            tally = jnp.sum(live, axis=0, keepdims=True)[:, 0:1]
            filled = (
                lax.broadcasted_iota(jnp.int32, (rows, 1), 0).astype(jnp.float32) < tally
            ).astype(jnp.float32)
        before = (rank_of(source, x) < rank_of(to, x)).astype(jnp.bfloat16)
        slot = jnp.dot(before, live.astype(jnp.bfloat16), preferred_element_type=jnp.float32)
        chooser = jnp.where(slot == source.astype(jnp.float32), live, 0.0).astype(jnp.bfloat16)
        target = lax.dot_general(
            chooser, block, (((0,), (0,)), ((), ())), preferred_element_type=jnp.float32
        )
        gain = gain_ref[:, span]
        normal = normal_ref[:, span]
        mismatch = (normal * gain - target) * filled
        weighted = mismatch * gain
        weighted_sum[:, span] = weighted
        row_terms += jnp.sum(weighted * normal, axis=1, keepdims=True)
        squares += jnp.sum(mismatch * mismatch, axis=1, keepdims=True)
        gain_sum[:, span] = jnp.sum(mismatch * normal, axis=0, keepdims=True)
    row_mean = row_terms * (1.0 / width)
    for span in spans:
        normal = normal_ref[:, span]
        gradient_ref[:, span] = (
            inverse_rms * (weighted_sum[:, span] - normal * row_mean)
        ).astype(jnp.bfloat16)
    share = width // mp_count
    square_sum = jnp.sum(squares, axis=0, keepdims=True)
    lane = lax.broadcasted_iota(jnp.int32, (1, message_ref.shape[2] - share), 1)
    tail = jnp.where(lane == 0, square_sum, jnp.where(lane == 1, tally, 0.0))
    for m in range(mp_count):
        message_ref[m, :, :share] = gain_sum[:, m * share : (m + 1) * share]
        message_ref[m, :, share:] = tail


def finish(received, normal, inverse_rms, gains, mp_count):
    rows, width = normal.shape
    share = width // mp_count
    in_vmem = pl.BlockSpec(memory_space=pltpu.VMEM)
    return pl.pallas_call(
        functools.partial(finish_kernel, mp_count),
        out_shape=(
            jax.ShapeDtypeStruct((rows, width), jnp.bfloat16),
            jax.ShapeDtypeStruct((mp_count, 1, share + 64), jnp.float32),
        ),
        in_specs=[in_vmem] * 4,
        out_specs=(in_vmem, in_vmem),
        scratch_shapes=[
            pltpu.VMEM((rows, width), jnp.float32),
            pltpu.VMEM((1, width), jnp.float32),
        ],
        compiler_params=pltpu.CompilerParams(vmem_limit_bytes=16 * MIB),
        cost_estimate=pl.CostEstimate(
            flops=2 * rows * rows * width, bytes_accessed=6 * rows * width, transcendentals=rows
        ),
    )(received, normal, inverse_rms, gains[None, :])


def last_kernel(share, width, parts_ref, gain_ref, loss_ref):
    total = jnp.sum(parts_ref[...], axis=0)
    tally = total[:, share + 1 : share + 2]
    gain_ref[...] = total[:, :share] / tally
    loss_ref[...] = total[:, share : share + 1] / (2.0 * tally * width)


def last(parts, share, width):
    in_vmem = pl.BlockSpec(memory_space=pltpu.VMEM)
    return pl.pallas_call(
        functools.partial(last_kernel, share, float(width)),
        out_shape=(
            jax.ShapeDtypeStruct((1, share), jnp.float32),
            jax.ShapeDtypeStruct((1, 1), jnp.float32),
        ),
        in_specs=[in_vmem],
        out_specs=(in_vmem, in_vmem),
        compiler_params=pltpu.CompilerParams(vmem_limit_bytes=4 * MIB),
    )(parts)


def ring_gather(top, low, x_count, dp_count):
    forward = [(d, d - d % x_count + (d + 1) % x_count) for d in range(dp_count)]
    backward = [(d, d - d % x_count + (d - 1) % x_count) for d in range(dp_count)]
    left_top = lax.ppermute(top, "dp", forward)
    right_low = lax.ppermute(low, "dp", backward)
    left_low = lax.ppermute(low, "dp", forward)
    right_top = lax.ppermute(top, "dp", backward)
    far_top = lax.ppermute(left_top, "dp", forward)
    far_low = lax.ppermute(right_low, "dp", backward)
    return [left_top, left_low, far_top, far_low, right_top, right_low]


def projector_columns(projector, student_gain, mp_count, x_count, y_count):
    core = lax.axis_index("group")
    dp_count = x_count * y_count
    columns = projector.T
    half, tile = columns.shape[0] // 2, columns.shape[1]
    share = lax.dynamic_slice_in_dim(columns, core * half, half, 0)
    moves = []
    for c in range(2):
        for d in range(dp_count):
            for z in range(mp_count):
                source = (c * dp_count + d) * mp_count + z
                y, x = divmod(d, x_count)
                to_d = y * x_count + z // 2
                moves.append((source, ((z % 2) * dp_count + to_d) * mp_count + 2 * x + c))
    piece = lax.ppermute(share, ("group", "dp", "mp"), moves)
    high = lax.reduce_precision(student_gain, 8, 7)
    middle = lax.reduce_precision(student_gain - high, 8, 7)
    low = student_gain - high - middle
    width = student_gain.shape[0]
    extra = 16
    parts = jnp.concatenate(
        [high, middle, low, jnp.zeros((extra * tile - 3 * width,), jnp.float32)]
    ).astype(jnp.bfloat16)
    message = jnp.concatenate([piece, parts.reshape(extra, tile)], axis=0)
    spread = lax.all_to_all(
        jnp.broadcast_to(message[None], (mp_count,) + message.shape), "mp", 0, 0, tiled=True
    )
    parts = spread[:, half:].reshape(mp_count, extra * tile).astype(jnp.float32)
    gains = parts[:, :width] + parts[:, width : 2 * width] + parts[:, 2 * width : 3 * width]
    tiles = spread.reshape(mp_count * (half + extra), tile)
    y_groups = [[y * x_count + x for y in range(y_count)] for x in range(x_count)]
    mine = lax.all_gather(tiles, "dp", axis=0, axis_index_groups=y_groups, tiled=True)
    return mine.reshape(y_count, mp_count, half + extra, tile), gains.reshape(mp_count * width)


def local(teacher_hidden, teacher_gain, projector, live, placement, student_hidden, student_gain):
    dp_count = lax.axis_size("dp")
    mp_count = lax.axis_size("mp")
    group_count = lax.axis_size("group")
    x_count = RING
    y_count = dp_count // x_count
    column = lax.axis_index("mp")
    core = lax.axis_index("group")
    slot_count = student_hidden.shape[0]
    capacity = slot_count // dp_count
    share_width = student_gain.shape[0]
    width = share_width * mp_count

    features = teacher_hidden.shape[1]
    blocks = teacher_hidden.reshape(mp_count, slot_count, features)
    moved = lax.all_to_all(blocks, "mp", 0, 0, tiled=True)
    mine, gains = projector_columns(projector, student_gain, mp_count, x_count, y_count)

    own_live = lax.dynamic_index_in_dim(live.reshape(mp_count, slot_count), column, 0, keepdims=False)
    own_shards = lax.dynamic_index_in_dim(placement.reshape(mp_count, slot_count), column, 0, keepdims=False)
    order = jnp.arange(slot_count, dtype=jnp.int32)
    same = (
        (own_shards[:, None] == own_shards[None, :])
        & (own_live[:, None] == 1)
        & (order[:, None] < order[None, :])
    )
    rank = jnp.sum(same.astype(jnp.int32), axis=0)
    slot = jnp.where(own_live == 1, rank * dp_count + own_shards, -1)

    top, low, own = norm_rows(moved, slot, teacher_gain)
    pieces = [own] + ring_gather(top, low, x_count, dp_count)
    mine, pieces = lax.optimization_barrier((mine, pieces))
    other = lax.ppermute(mine, "group", [(0, 1), (1, 0)])
    half = share_width // 2
    first = product(pieces, mine, half, dp_count)
    place = core.astype(jnp.int32).reshape(1)
    buffer = product(pieces, other, half, dp_count, place, first)
    quarter = buffer.shape[1]
    deep = x_count * capacity
    received = lax.all_to_all(
        buffer.reshape(dp_count, deep, quarter), "dp", 0, 0, tiled=True
    ).reshape(y_count, x_count, deep, quarter)
    hidden, _ = lax.optimization_barrier((student_hidden, buffer))
    normal, inverse_rms = student_rows(hidden)
    gradient, message = finish(received, normal, inverse_rms, gains, mp_count)

    over_mp = jnp.sum(lax.all_to_all(message, "mp", 0, 0, tiled=True), axis=(0, 1))
    peers = group_count * dp_count
    parts = lax.all_to_all(
        jnp.broadcast_to(over_mp[None, None, :], (peers, 1, over_mp.shape[0])),
        ("group", "dp"),
        0,
        0,
        tiled=True,
    )
    grad_gain, mean_loss = last(parts, share_width, width)
    return (gradient, grad_gain.reshape(share_width), mean_loss.reshape(()))


def solution(mesh):
    placed = (
        P(("group", "dp"), "mp"),
        P(),
        P("dp", "mp"),
        P(("group", "dp")),
        P(("group", "dp")),
        P(("group", "dp", "mp"), None),
        P("mp"),
    )
    return jax.shard_map(
        local,
        mesh=mesh,
        in_specs=placed,
        out_specs=(P(("group", "dp", "mp"), None), P("mp"), P()),
        check_vma=False,
    )
```

```python
import functools

import jax
import jax.numpy as jnp
from jax import lax
from jax.experimental import pallas as pl
from jax.experimental.pallas import tpu as pltpu
from jax.sharding import PartitionSpec as P

EPSILON = 1e-06
RING = 4
MIB = 1024 * 1024
EMPTY = 1e30
EMPTY_FROM = 1e20


def norm_kernel(moved_ref, slot_ref, gain_ref, top_ref, low_ref, packed):
    parts, rows, features = moved_ref.shape
    order = lax.broadcasted_iota(jnp.int32, (rows, rows), 0)
    packer = (order == slot_ref[...]).astype(jnp.bfloat16)
    total = jnp.zeros((rows, 1), jnp.float32)
    for part in range(parts):
        values = jnp.dot(packer, moved_ref[part], preferred_element_type=jnp.float32)
        packed[part] = values
        total += jnp.sum(values * values, axis=1, keepdims=True)
    inverse_rms = lax.rsqrt(total * (1.0 / (parts * features)) + EPSILON)
    half = rows // 2
    taken = jnp.sum(packer.astype(jnp.float32), axis=1, keepdims=True)
    first_column = lax.broadcasted_iota(jnp.int32, (rows, features), 1) == 0
    for part in range(parts):
        columns = slice(part * features, (part + 1) * features)
        normed = packed[part] * inverse_rms * gain_ref[:, columns]
        if part == 0:
            normed = jnp.where(first_column & (taken == 0.0), EMPTY, normed)
        normed = normed.astype(jnp.bfloat16)
        top_ref[:, columns] = normed[:half]
        low_ref[:, columns] = normed[half:]


def norm_rows(moved, slot, teacher_gain):
    parts, rows, features = moved.shape
    half = jax.ShapeDtypeStruct((rows // 2, parts * features), jnp.bfloat16)
    return pl.pallas_call(
        norm_kernel,
        out_shape=(half, half),
        scratch_shapes=[pltpu.VMEM((parts, rows, features), jnp.float32)],
        compiler_params=pltpu.CompilerParams(vmem_limit_bytes=16 * MIB),
        cost_estimate=pl.CostEstimate(
            flops=2 * rows * rows * parts * features,
            bytes_accessed=4 * rows * parts * features,
            transcendentals=rows,
        ),
    )(moved, slot[None, :], teacher_gain[None, :])


def block_dot(rows, weights, half, spans, pairs):
    tile = weights.shape[3]
    tiles = [
        weights[span, 2 * pair : 2 * pair + 2, :half].reshape(2 * half, tile)
        for span in spans
        for pair in range(pairs)
    ]
    return lax.dot_general(
        rows,
        jnp.concatenate(tiles, axis=1),
        (((1,), (1,)), ((), ())),
        preferred_element_type=jnp.float32,
    )


def block_product(pieces, weights, half, total):
    y_count, shares = weights.shape[:2]
    steps = 4
    spans = y_count // steps
    part = pieces[0].shape[1] // steps
    for step in range(steps):
        features = slice(step * part, (step + 1) * part)
        partial = block_dot(
            jnp.concatenate([piece[:, features] for piece in pieces], axis=0),
            weights,
            half,
            range(step * spans, (step + 1) * spans),
            shares // 2,
        )
        if step == 0:
            total[...] = partial
        else:
            total[...] += partial


def turned(shards, total, pieces):
    rows = total.shape[0]
    depth = rows // shards
    to = lax.broadcasted_iota(jnp.int32, (rows, rows), 0)
    source = lax.broadcasted_iota(jnp.int32, (rows, rows), 1)
    turn = (source == (to % depth) * shards + to // depth).astype(jnp.bfloat16)
    first_features = jnp.concatenate([piece[:, :128] for piece in pieces], axis=0)
    empty = first_features.astype(jnp.float32)[:, 0:1] > EMPTY_FROM
    kept = jnp.where(empty, EMPTY, total[...]).astype(jnp.bfloat16)
    return jnp.dot(turn, kept, preferred_element_type=jnp.float32).astype(jnp.bfloat16)


def first_kernel(shards, half, count, *refs):
    pieces, weights_ref, out_ref, total = refs[:count], *refs[count:]
    block_product(pieces, weights_ref, half, total)
    out_ref[...] = turned(shards, total, pieces)


def second_kernel(shards, half, count, core_ref, first_ref, *refs):
    pieces, weights_ref, out_ref, total = refs[:count], *refs[count:]
    block_product(pieces, weights_ref, half, total)
    width = total.shape[1]
    mine = first_ref[...]
    other = turned(shards, total, pieces)

    @pl.when(core_ref[0] == 0)
    def _():
        out_ref[:, :width] = mine
        out_ref[:, width:] = other

    @pl.when(core_ref[0] != 0)
    def _():
        out_ref[:, :width] = other
        out_ref[:, width:] = mine


def product(pieces, weights, half, shards, core=None, first=None):
    y_count, shares, _, tile = weights.shape
    depth = y_count * (shares // 2) * tile
    count = len(pieces)
    total_rows = pieces[0].shape[0] * count
    joined = first is not None
    in_vmem = pl.BlockSpec(memory_space=pltpu.VMEM)
    head = [pl.BlockSpec(memory_space=pltpu.SMEM), in_vmem] if joined else []
    kernel = second_kernel if joined else first_kernel
    return pl.pallas_call(
        functools.partial(kernel, shards, half, count),
        out_shape=jax.ShapeDtypeStruct(
            (total_rows, (4 if joined else 2) * half), jnp.bfloat16
        ),
        in_specs=head + [in_vmem] * (count + 1),
        out_specs=in_vmem,
        scratch_shapes=[pltpu.VMEM((total_rows, 2 * half), jnp.float32)],
        compiler_params=pltpu.CompilerParams(vmem_limit_bytes=32 * MIB),
        cost_estimate=pl.CostEstimate(
            flops=4 * total_rows * depth * half,
            bytes_accessed=2 * depth * (total_rows + 2 * half),
            transcendentals=0,
        ),
    )(*((core, first) if joined else ()), *pieces, weights)


def student_kernel(hidden_ref, normal_ref, rms_ref):
    rows, width = hidden_ref.shape
    quarter = width // 4
    spans = [slice(x * quarter, (x + 1) * quarter) for x in range(4)]
    total = jnp.zeros((rows, 1), jnp.float32)
    for span in spans:
        values = hidden_ref[:, span].astype(jnp.float32)
        total += jnp.sum(values * values, axis=1, keepdims=True)
    inverse_rms = lax.rsqrt(total * (1.0 / width) + EPSILON)
    for span in spans:
        normal_ref[:, span] = hidden_ref[:, span].astype(jnp.float32) * inverse_rms
    rms_ref[...] = jnp.broadcast_to(inverse_rms, rms_ref.shape)


def student_rows(hidden):
    rows, width = hidden.shape
    in_vmem = pl.BlockSpec(memory_space=pltpu.VMEM)
    return pl.pallas_call(
        student_kernel,
        out_shape=(
            jax.ShapeDtypeStruct((rows, width), jnp.float32),
            jax.ShapeDtypeStruct((rows, 128), jnp.float32),
        ),
        in_specs=[in_vmem],
        out_specs=(in_vmem, in_vmem),
        compiler_params=pltpu.CompilerParams(vmem_limit_bytes=16 * MIB),
        cost_estimate=pl.CostEstimate(
            flops=4 * rows * width, bytes_accessed=6 * rows * width, transcendentals=rows
        ),
    )(hidden)


def student_parts(received_ref, normal_ref, gain_ref):
    y_count, x_count, deep, quarter = received_ref.shape
    rows = normal_ref.shape[0]
    capacity = deep // x_count
    to = lax.broadcasted_iota(jnp.int32, (rows, rows), 0)
    source = lax.broadcasted_iota(jnp.int32, (rows, rows), 1)

    def rank_of(row, x):
        y, j, rank = row // deep, (row // capacity) % x_count, row % capacity
        return (y * x_count + (x - j + x_count) % x_count) * capacity + rank

    parts = []
    tally = None
    for x in range(x_count):
        span = slice(x * quarter, (x + 1) * quarter)
        block = received_ref[:, x].reshape(y_count * deep, quarter)
        live = jnp.where(block[:, 0:1].astype(jnp.float32) < EMPTY_FROM, 1.0, 0.0)
        live = jnp.broadcast_to(live, (rows, rows))
        if tally is None:
            tally = jnp.sum(live, axis=0, keepdims=True)[:, 0:1]
            filled = (
                lax.broadcasted_iota(jnp.int32, (rows, 1), 0).astype(jnp.float32) < tally
            ).astype(jnp.float32)
        before = (rank_of(source, x) < rank_of(to, x)).astype(jnp.bfloat16)
        slot = jnp.dot(before, live.astype(jnp.bfloat16), preferred_element_type=jnp.float32)
        chooser = jnp.where(slot == source.astype(jnp.float32), live, 0.0).astype(jnp.bfloat16)
        target = lax.dot_general(
            chooser, block, (((0,), (0,)), ((), ())), preferred_element_type=jnp.float32
        )
        gain = gain_ref[:, span]
        normal = normal_ref[:, span]
        parts.append((span, normal, gain, (normal * gain - target) * filled))
    return parts, tally


def message_kernel(mp_count, received_ref, normal_ref, gain_ref, message_ref, gain_sum):
    rows, width = normal_ref.shape
    parts, tally = student_parts(received_ref, normal_ref, gain_ref)
    squares = jnp.zeros((rows, 1), jnp.float32)
    for span, normal, _, mismatch in parts:
        squares += jnp.sum(mismatch * mismatch, axis=1, keepdims=True)
        gain_sum[:, span] = jnp.sum(mismatch * normal, axis=0, keepdims=True)
    share = width // mp_count
    square_sum = jnp.sum(squares, axis=0, keepdims=True)
    lane = lax.broadcasted_iota(jnp.int32, (1, message_ref.shape[2] - share), 1)
    tail = jnp.where(lane == 0, square_sum, jnp.where(lane == 1, tally, 0.0))
    for m in range(mp_count):
        message_ref[m, :, :share] = gain_sum[:, m * share : (m + 1) * share]
        message_ref[m, :, share:] = tail


def gradient_kernel(received_ref, normal_ref, rms_ref, gain_ref, gradient_ref, weighted_sum):
    rows, width = normal_ref.shape
    parts, _ = student_parts(received_ref, normal_ref, gain_ref)
    row_terms = jnp.zeros((rows, 1), jnp.float32)
    for span, normal, gain, mismatch in parts:
        weighted = mismatch * gain
        weighted_sum[:, span] = weighted
        row_terms += jnp.sum(weighted * normal, axis=1, keepdims=True)
    row_mean = row_terms * (1.0 / width)
    for span, _, _, _ in parts:
        gradient_ref[:, span] = (
            rms_ref[:, 0:1] * (weighted_sum[:, span] - normal_ref[:, span] * row_mean)
        ).astype(jnp.bfloat16)


def finish(received, normal, gains, mp_count):
    rows, width = normal.shape
    share = width // mp_count
    in_vmem = pl.BlockSpec(memory_space=pltpu.VMEM)
    cost = pl.CostEstimate(
        flops=2 * rows * rows * width, bytes_accessed=6 * rows * width, transcendentals=0
    )
    message = pl.pallas_call(
        functools.partial(message_kernel, mp_count),
        out_shape=jax.ShapeDtypeStruct((mp_count, 1, share + 64), jnp.float32),
        in_specs=[in_vmem] * 3,
        out_specs=in_vmem,
        scratch_shapes=[pltpu.VMEM((1, width), jnp.float32)],
        compiler_params=pltpu.CompilerParams(vmem_limit_bytes=16 * MIB),
        cost_estimate=cost,
    )(received, normal, gains[None, :])
    return message


def student_gradient(received, normal, inverse_rms, gains):
    rows, width = normal.shape
    in_vmem = pl.BlockSpec(memory_space=pltpu.VMEM)
    return pl.pallas_call(
        gradient_kernel,
        out_shape=jax.ShapeDtypeStruct((rows, width), jnp.bfloat16),
        in_specs=[in_vmem] * 4,
        out_specs=in_vmem,
        scratch_shapes=[pltpu.VMEM((rows, width), jnp.float32)],
        compiler_params=pltpu.CompilerParams(vmem_limit_bytes=16 * MIB),
        cost_estimate=pl.CostEstimate(
            flops=2 * rows * rows * width, bytes_accessed=6 * rows * width, transcendentals=0
        ),
    )(received, normal, inverse_rms, gains[None, :])


def last_kernel(share, width, parts_ref, gain_ref, loss_ref):
    total = jnp.sum(parts_ref[...], axis=0)
    tally = total[:, share + 1 : share + 2]
    gain_ref[...] = total[:, :share] / tally
    loss_ref[...] = total[:, share : share + 1] / (2.0 * tally * width)


def last(parts, share, width):
    in_vmem = pl.BlockSpec(memory_space=pltpu.VMEM)
    return pl.pallas_call(
        functools.partial(last_kernel, share, float(width)),
        out_shape=(
            jax.ShapeDtypeStruct((1, share), jnp.float32),
            jax.ShapeDtypeStruct((1, 1), jnp.float32),
        ),
        in_specs=[in_vmem],
        out_specs=(in_vmem, in_vmem),
        compiler_params=pltpu.CompilerParams(vmem_limit_bytes=4 * MIB),
    )(parts)


def ring_gather(top, low, x_count, dp_count):
    forward = [(d, d - d % x_count + (d + 1) % x_count) for d in range(dp_count)]
    backward = [(d, d - d % x_count + (d - 1) % x_count) for d in range(dp_count)]
    left_top = lax.ppermute(top, "dp", forward)
    right_low = lax.ppermute(low, "dp", backward)
    left_low = lax.ppermute(low, "dp", forward)
    right_top = lax.ppermute(top, "dp", backward)
    far_top = lax.ppermute(left_top, "dp", forward)
    far_low = lax.ppermute(right_low, "dp", backward)
    return [top, low, left_top, left_low, far_top, far_low, right_top, right_low]


def projector_columns(projector, student_gain, mp_count, x_count, y_count):
    core = lax.axis_index("group")
    dp_count = x_count * y_count
    columns = projector.T
    half, tile = columns.shape[0] // 2, columns.shape[1]
    share = lax.dynamic_slice_in_dim(columns, core * half, half, 0)
    moves = []
    for c in range(2):
        for d in range(dp_count):
            for z in range(mp_count):
                source = (c * dp_count + d) * mp_count + z
                y, x = divmod(d, x_count)
                to_d = y * x_count + z // 2
                moves.append((source, ((z % 2) * dp_count + to_d) * mp_count + 2 * x + c))
    piece = lax.ppermute(share, ("group", "dp", "mp"), moves)
    high = lax.reduce_precision(student_gain, 8, 7)
    middle = lax.reduce_precision(student_gain - high, 8, 7)
    low = student_gain - high - middle
    width = student_gain.shape[0]
    extra = 16
    parts = jnp.concatenate(
        [high, middle, low, jnp.zeros((extra * tile - 3 * width,), jnp.float32)]
    ).astype(jnp.bfloat16)
    message = jnp.concatenate([piece, parts.reshape(extra, tile)], axis=0)
    spread = lax.all_to_all(
        jnp.broadcast_to(message[None], (mp_count,) + message.shape), "mp", 0, 0, tiled=True
    )
    parts = spread[:, half:].reshape(mp_count, extra * tile).astype(jnp.float32)
    gains = parts[:, :width] + parts[:, width : 2 * width] + parts[:, 2 * width : 3 * width]
    tiles = spread.reshape(mp_count * (half + extra), tile)
    y_groups = [[y * x_count + x for y in range(y_count)] for x in range(x_count)]
    mine = lax.all_gather(tiles, "dp", axis=0, axis_index_groups=y_groups, tiled=True)
    return mine.reshape(y_count, mp_count, half + extra, tile), gains.reshape(mp_count * width)


def local(teacher_hidden, teacher_gain, projector, live, placement, student_hidden, student_gain):
    dp_count = lax.axis_size("dp")
    mp_count = lax.axis_size("mp")
    group_count = lax.axis_size("group")
    x_count = RING
    y_count = dp_count // x_count
    column = lax.axis_index("mp")
    core = lax.axis_index("group")
    slot_count = student_hidden.shape[0]
    capacity = slot_count // dp_count
    share_width = student_gain.shape[0]
    width = share_width * mp_count

    features = teacher_hidden.shape[1]
    blocks = teacher_hidden.reshape(mp_count, slot_count, features)
    moved = lax.all_to_all(blocks, "mp", 0, 0, tiled=True)
    mine, gains = projector_columns(projector, student_gain, mp_count, x_count, y_count)

    own_live = lax.dynamic_index_in_dim(live.reshape(mp_count, slot_count), column, 0, keepdims=False)
    own_shards = lax.dynamic_index_in_dim(placement.reshape(mp_count, slot_count), column, 0, keepdims=False)
    order = jnp.arange(slot_count, dtype=jnp.int32)
    same = (
        (own_shards[:, None] == own_shards[None, :])
        & (own_live[:, None] == 1)
        & (order[:, None] < order[None, :])
    )
    rank = jnp.sum(same.astype(jnp.int32), axis=0)
    slot = jnp.where(own_live == 1, rank * dp_count + own_shards, -1)

    top, low = norm_rows(moved, slot, teacher_gain)
    pieces = ring_gather(top, low, x_count, dp_count)
    mine, pieces = lax.optimization_barrier((mine, pieces))
    other = lax.ppermute(mine, "group", [(0, 1), (1, 0)])
    half = share_width // 2
    first = product(pieces, mine, half, dp_count)
    place = core.astype(jnp.int32).reshape(1)
    buffer = product(pieces, other, half, dp_count, place, first)
    quarter = buffer.shape[1]
    deep = x_count * capacity
    received = lax.all_to_all(
        buffer.reshape(dp_count, deep, quarter), "dp", 0, 0, tiled=True
    ).reshape(y_count, x_count, deep, quarter)
    hidden, _ = lax.optimization_barrier((student_hidden, buffer))
    normal, inverse_rms = student_rows(hidden)
    message = finish(received, normal, gains, mp_count)

    over_mp = jnp.sum(lax.all_to_all(message, "mp", 0, 0, tiled=True), axis=(0, 1))
    received, _ = lax.optimization_barrier((received, over_mp))
    gradient = student_gradient(received, normal, inverse_rms, gains)
    peers = group_count * dp_count
    parts = lax.all_to_all(
        jnp.broadcast_to(over_mp[None, None, :], (peers, 1, over_mp.shape[0])),
        ("group", "dp"),
        0,
        0,
        tiled=True,
    )
    grad_gain, mean_loss = last(parts, share_width, width)
    return (gradient, grad_gain.reshape(share_width), mean_loss.reshape(()))


def solution(mesh):
    placed = (
        P(("group", "dp"), "mp"),
        P(),
        P("dp", "mp"),
        P(("group", "dp")),
        P(("group", "dp")),
        P(("group", "dp", "mp"), None),
        P("mp"),
    )
    return jax.shard_map(
        local,
        mesh=mesh,
        in_specs=placed,
        out_specs=(P(("group", "dp", "mp"), None), P("mp"), P()),
        check_vma=False,
    )
```
